128 devices in a mesh: dp: 8 (over y, z_hi), ctx: 16 (over x, z_lo, core).
Axes of the slice: x: 4, y: 4, z: 4 (z_hi: 2, z_lo: 2; z = z_hi * 2 + z_lo), core: 2. Of those that a mesh axis runs over, the one named last changes fastest.
Arguments:
- queries: bfloat16 [8, 4096, 2048], P('dp', 'ctx'), may hold values from -6 to 6
- keys: bfloat16 [8, 4096, 2048], P('dp', 'ctx'), may hold values from -6 to 6
- values: bfloat16 [8, 4096, 2048], P('dp', 'ctx'), may hold values from -6 to 6
- out_grad: bfloat16 [8, 4096, 2048], P('dp', 'ctx'), may hold values from -96 to 96
- layer_input: bfloat16 [8, 4096, 2048], P('dp', 'ctx'), may hold values from -6 to 6
- global_blocks: int32 [8, 2], P('dp'), may hold values from 0 to 31, as said below
- random_blocks: int32 [8, 32, 3], P('dp'), may hold values from 0 to 31, as said below
Outputs:
- query_grad: bfloat16 [8, 4096, 2048], P('dp', 'ctx')
- key_grad: bfloat16 [8, 4096, 2048], P('dp', 'ctx')
- value_grad: bfloat16 [8, 4096, 2048], P('dp', 'ctx')
- value_weight_grad: float32 [2048, 2048], P(('dp', 'ctx'))
The draws below stay inside these ranges and needn't reach their ends.
Inputs may be any that keep to these rules, and one draw needn't show every extreme that they name: `global_blocks`: for each document, 2 distinct blocks. `random_blocks`: for each document and query block b, 3 distinct blocks, none of them b-1, b, b+1 or a global block of that document.
All inputs are finite; a program needn't handle non-finite values.
Results may differ from the reference program's by a relative error of at most 0.018.
Values may be sent and summed in bfloat16 or wider, within the bound.
No kernel may reach another device: no remote copies, remote signals or barrier semaphores. Data moves between devices by JAX's collectives and lax.ppermute only.
A program may use at most 128 MiB of HBM per device.

```python
import math
import jax
import jax.numpy as jnp
from jax import lax

HEADS = 16
HEAD_DIM = 128
DX = 2048
BLOCK = 128
GLOBAL = 2
RANDOM = 3
SEQ = 4096
NB = 32
HD = 2048
N_DP = 8


def pick_globals(key):
    split_keys = jax.random.split(key, N_DP + 2)
    chosen = jax.vmap(lambda single: jax.random.permutation(single, NB)[:GLOBAL])(split_keys[:N_DP])
    inner = jax.random.permutation(split_keys[N_DP], NB - 2)[:GLOBAL] + 1
    slots = jnp.arange(GLOBAL)
    edge_row = jnp.where(slots == 0, NB - 1, jnp.where(slots == 1, 0, inner))
    special = jax.random.randint(split_keys[N_DP + 1], (), 0, N_DP)
    docs = jnp.arange(N_DP)
    chosen = jnp.where((docs == special)[:, None], edge_row[None, :], chosen)
    return chosen.astype(jnp.int32)


def draw_global_blocks(key, part):
    return pick_globals(key)


def draw_random_blocks(key, part):
    own_key = jax.random.fold_in(key, 7)
    chosen_globals = pick_globals(key)
    candidates = jnp.arange(NB, dtype=jnp.int32)
    scores = jax.random.randint(own_key, (N_DP, NB, NB), 0, 1 << 20) * NB + candidates[None, None, :]
    nearby = jnp.abs(candidates[None, :] - candidates[:, None]) <= 1
    is_global = jnp.any(candidates[None, None, :] == chosen_globals[:, :, None], axis=1)
    banned = nearby[None, :, :] | is_global[:, None, :]
    scores = jnp.where(banned, -1, scores)
    unused_values, picks = lax.top_k(scores, RANDOM)
    return picks.astype(jnp.int32)


def draw_queries(key, part):
    own_key = jax.random.fold_in(key, 11)
    result = jnp.clip(jax.random.normal(own_key, (N_DP, SEQ, HD), jnp.float32), -6.0, 6.0)
    return result.astype(jnp.bfloat16)


def draw_keys(key, part):
    own_key = jax.random.fold_in(key, 13)
    result = jnp.clip(jax.random.normal(own_key, (N_DP, SEQ, HD), jnp.float32), -6.0, 6.0)
    return result.astype(jnp.bfloat16)


def spiked(values, rng, source, target, blocks, factor):
    owner, partner = [(jnp.arange(values.shape[dim]) // (values.shape[dim] // blocks)).reshape([-1 if axis == dim else 1 for axis in range(values.ndim)]) for dim in (source, target)]
    chosen = jax.random.permutation(rng, blocks)[partner]
    strong = (owner == chosen) | (owner == (partner + blocks // 2) % blocks)
    return jnp.where(strong, factor * values, values)


def steps_of(rng, shape, pieces, smallest, top_value):
    level, own = 1.0, jax.random.fold_in(rng, 6)
    for position, blocks in pieces:
        draws = jnp.exp(jax.random.uniform(jax.random.fold_in(own, position), (blocks,), jnp.float32, smallest / len(pieces), top_value / len(pieces)))
        level = level * jnp.repeat(draws, shape[position] // blocks).reshape([-1 if axis == position else 1 for axis in range(len(shape))])
    return level


def scatter_about(stream_key, extent, width, most, pieces=(), kind=jnp.bfloat16):
    entries = jax.random.normal(stream_key, extent, jnp.float32) * width
    if len(pieces) > 0:
        entries = steps_of(stream_key, extent, pieces, -0.22, 0.18) * entries
    return jnp.clip(entries, min=-most, max=most).astype(kind)


def noise_with(stream_key, shape, scale, bound, shards, heavy, kind=jnp.bfloat16):
    values = scale * jax.random.normal(stream_key, shape, jnp.float32)
    if shards:
        values = values * steps_of(stream_key, shape, shards, -0.22, 0.18)
    return jnp.clip(spiked(values, jax.random.fold_in(stream_key, 3), *heavy), -bound, bound).astype(kind)


def setup_inputs(seed: int = 0) -> dict:
    key_list = jax.random.split(jax.random.key(seed), 8)
    queries = draw_queries(jax.random.fold_in(key_list[7], 71), 0)
    keys = draw_keys(jax.random.fold_in(key_list[7], 71), 0)
    values = scatter_about(key_list[2], (N_DP, SEQ, HD), 1.0, 6.0, ((0, 8), (1, 16)))
    out_grad = scatter_about(key_list[3], (N_DP, SEQ, HD), 16.0, 96.0, ((0, 8), (1, 16)))
    layer_input = noise_with(key_list[4], (N_DP, SEQ, DX), 1.0, 6.0, ((0, 8), (1, 16)), (1, 2, 16, 2.0))
    global_blocks = draw_global_blocks(jax.random.fold_in(key_list[7], 71), 0)
    random_blocks = draw_random_blocks(jax.random.fold_in(key_list[7], 71), 0)
    return {"queries": queries, "keys": keys, "values": values, "out_grad": out_grad, "layer_input": layer_input, "global_blocks": global_blocks, "random_blocks": random_blocks}


def block_table(global_row, random_rows, block_count):
    blocks = jnp.arange(block_count, dtype=jnp.int32)
    left_side = blocks - 1
    right_side = blocks + 1
    global_wide = jnp.broadcast_to(global_row[None, :].astype(jnp.int32), (block_count, global_row.shape[0]))
    table = jnp.concatenate([left_side[:, None], blocks[:, None], right_side[:, None], global_wide, random_rows.astype(jnp.int32)], axis=1)
    counted = jnp.concatenate([(left_side >= 0)[:, None], jnp.ones((block_count, 1), jnp.bool_), (right_side < block_count)[:, None], jnp.abs(global_wide - blocks[:, None]) > 1, jnp.ones(random_rows.shape, jnp.bool_)], axis=1)
    return (jnp.clip(table, 0, block_count - 1).astype(jnp.int32), counted)

def group_probs(query_tile, key_tile, counted_tile, scale):
    scores = jnp.einsum('gihe,gjkhe->ghijk', query_tile.astype(jnp.float32), key_tile.astype(jnp.float32)) * scale
    scores = jnp.where(counted_tile[:, None, None, :, None], scores, -jnp.inf)
    largest = lax.optimization_barrier(jnp.max(scores, axis=(3, 4), keepdims=True))
    weights = jnp.exp(scores - largest)
    probs = weights / lax.optimization_barrier(jnp.sum(weights, axis=(3, 4), keepdims=True))
    return (probs, probs.astype(jnp.bfloat16))

def group_grads(probs, probs_low, query_tile, key_tile, value_tile, grad_tile, scale):
    attn_out = jnp.einsum('ghijk,gjkhe->gihe', probs_low.astype(jnp.float32), value_tile.astype(jnp.float32))
    delta = lax.optimization_barrier(jnp.sum(grad_tile.astype(jnp.float32) * attn_out, axis=-1))
    value_part = jnp.einsum('ghijk,gihe->gjkhe', probs_low.astype(jnp.float32), grad_tile.astype(jnp.float32))
    dprobs = jnp.einsum('gihe,gjkhe->ghijk', grad_tile.astype(jnp.float32), value_tile.astype(jnp.float32))
    centered = dprobs - jnp.transpose(delta, (0, 2, 1))[:, :, :, None, None]
    dscore = (probs * centered * scale).astype(jnp.bfloat16)
    query_part = jnp.einsum('ghijk,gjkhe->gihe', dscore.astype(jnp.float32), key_tile.astype(jnp.float32)).astype(jnp.bfloat16)
    key_part = jnp.einsum('ghijk,gihe->gjkhe', dscore.astype(jnp.float32), query_tile.astype(jnp.float32))
    return (query_part, key_part, value_part)

def sparse_grads(query4, key4, value4, grad4, table, counted):
    block_count, block_rows = (query4.shape[0], query4.shape[1])
    per_step = min(block_count, max(1, 512 // block_rows))
    step_count = block_count // per_step
    scale = 1.0 / math.sqrt(query4.shape[3])

    def advance(carry, index):
        key_acc, value_acc = carry
        first = (index * per_step).astype(jnp.int32)
        query_tile = lax.dynamic_slice_in_dim(query4, first, per_step, 0)
        grad_tile = lax.dynamic_slice_in_dim(grad4, first, per_step, 0)
        picks = lax.dynamic_slice_in_dim(table, first, per_step, 0)
        counted_tile = lax.dynamic_slice_in_dim(counted, first, per_step, 0)
        key_tile = key4[picks]
        value_tile = value4[picks]
        probs, probs_low = group_probs(query_tile, key_tile, counted_tile, scale)
        query_part, key_part, value_part = group_grads(probs, probs_low, query_tile, key_tile, value_tile, grad_tile, scale)
        return ((key_acc.at[picks].add(key_part), value_acc.at[picks].add(value_part)), query_part)
    zeros = jnp.zeros(query4.shape, jnp.float32)
    (key_acc, value_acc), query_parts = lax.scan(advance, (zeros, zeros), jnp.arange(step_count, dtype=jnp.int32))
    return (query_parts.reshape(query4.shape), key_acc.astype(jnp.bfloat16), value_acc.astype(jnp.bfloat16))

def one_document(packed):
    query_doc, key_doc, value_doc, grad_doc, global_row, random_rows = packed
    shape4 = (NB, BLOCK, HEADS, HEAD_DIM)
    table, counted = block_table(global_row, random_rows, NB)
    query_part, key_part, value_part = sparse_grads(query_doc.reshape(shape4), key_doc.reshape(shape4), value_doc.reshape(shape4), grad_doc.reshape(shape4), table, counted)
    return (query_part.reshape(SEQ, HD), key_part.reshape(SEQ, HD), value_part.reshape(SEQ, HD))

def reference(queries, keys, values, out_grad, layer_input, global_blocks, random_blocks):
    query_grad, key_grad, value_grad = lax.map(one_document, (queries, keys, values, out_grad, global_blocks, random_blocks))
    total = jnp.zeros((DX, HD), jnp.float32)
    for replica in range(N_DP):
        total = total + jnp.dot(layer_input[replica].T, value_grad[replica], preferred_element_type=jnp.float32)
    value_weight_grad = total / math.sqrt(N_DP * SEQ)
    return (query_grad, key_grad, value_grad, value_weight_grad)
```

```python
import functools
import math

import jax
import jax.numpy as jnp
from jax import lax
from jax.experimental import pallas as pl
from jax.experimental.pallas import tpu as pltpu
from jax.sharding import Mesh, PartitionSpec as P

D = 128
BLOCK = 128
F32 = jnp.float32
BF16 = jnp.bfloat16
LOG2E = 1.4426950408889634
DP = ("y", "zh")
CTX = ("x", "zl", "core")
NEG = float("-inf")


def pack_kernel(groups, *refs):
    count = sum(groups)
    ins, outs = refs[:count], refs[count:]
    first = 0
    for out, size in zip(outs, groups):
        rows = ins[first].shape[1]
        for n in range(size):
            for h in range(out.shape[0]):
                out[h, n * rows : (n + 1) * rows, :] = ins[first + n][0, :, h * D : (h + 1) * D]
        first += size


def pack(*groups):
    flat = [a for group in groups for a in group]
    rows, cols = flat[0].shape[1:]
    heads = cols // D
    return pl.pallas_call(
        functools.partial(pack_kernel, tuple(len(group) for group in groups)),
        out_shape=[
            jax.ShapeDtypeStruct((heads, len(group) * rows, D), BF16) for group in groups
        ],
        in_specs=[pl.BlockSpec(memory_space=pltpu.VMEM)] * len(flat),
        out_specs=[pl.BlockSpec(memory_space=pltpu.VMEM)] * len(groups),
        compiler_params=pltpu.CompilerParams(vmem_limit_bytes=24 * 1024 * 1024),
        name="pack",
        cost_estimate=pl.CostEstimate(
            flops=0, bytes_accessed=4 * rows * cols * len(flat), transcendentals=0
        ),
    )(*flat)


def unpack_kernel(count, src, *outs):
    rows = outs[0].shape[1]
    for n, out in enumerate(outs):
        for h in range(src.shape[0]):
            out[0, :, h * D : (h + 1) * D] = src[h, n * rows : (n + 1) * rows, :]


def unpack(array, count):
    heads, rows = array.shape[0], array.shape[1] // count
    return pl.pallas_call(
        functools.partial(unpack_kernel, count),
        out_shape=[jax.ShapeDtypeStruct((1, rows, heads * D), BF16)] * count,
        in_specs=[pl.BlockSpec(memory_space=pltpu.VMEM)],
        out_specs=[pl.BlockSpec(memory_space=pltpu.VMEM)] * count,
        compiler_params=pltpu.CompilerParams(vmem_limit_bytes=24 * 1024 * 1024),
        name="unpack",
        cost_estimate=pl.CostEstimate(
            flops=0, bytes_accessed=4 * rows * heads * D * count, transcendentals=0
        ),
    )(array)


def table_row(glob_ref, rand_ref, b, nb):
    left, right = b - 1, b + 1
    g0, g1 = glob_ref[0, 0], glob_ref[0, 1]
    idx = [
        jnp.maximum(left, 0),
        b,
        jnp.minimum(right, nb - 1),
        g0,
        g1,
        rand_ref[0, b, 0],
        rand_ref[0, b, 1],
        rand_ref[0, b, 2],
    ]

    def bias(c):
        return jnp.where(c, 0.0, NEG).astype(F32)

    biases = [
        bias(left >= 0),
        None,
        bias(right < nb),
        bias(jnp.abs(g0 - b) > 1),
        bias(jnp.abs(g1 - b) > 1),
        None,
        None,
        None,
    ]
    return idx, biases


def nt(a, b):
    return lax.dot_general(a, b, (((1,), (1,)), ((), ())), preferred_element_type=F32)


def probs_kernel(nb, scale, glob_ref, rand_ref, q_ref, k_ref, g_ref, p_ref, dv_ref, acc):
    step = pl.program_id(0)
    per = q_ref.shape[1]

    @pl.when(step == 0)
    def _():
        acc[...] = jnp.zeros_like(acc)

    for u in range(per):
        b = step * per + u
        idx, biases = table_row(glob_ref, rand_ref, b, nb)
        keys = jnp.concatenate([k_ref[i // 2, i % 2] for i in idx], axis=0)
        s = nt(q_ref[0, u], keys)
        tiles = [s[:, j * D : (j + 1) * D] for j in range(8)]
        tiles = [t if c is None else t + c for t, c in zip(tiles, biases)]
        top = functools.reduce(jnp.maximum, tiles)
        top = jnp.max(top, axis=1, keepdims=True)
        c2 = scale * LOG2E
        e = [jnp.exp2((t - top) * c2) for t in tiles]
        total = jnp.sum(functools.reduce(jnp.add, e), axis=1, keepdims=True)
        inv = 1.0 / total
        p = jnp.concatenate([(t * inv).astype(BF16) for t in e], axis=1)
        p_ref[u] = p
        part = jnp.dot(g_ref[0, u].T, p, preferred_element_type=F32)
        for j, i in enumerate(idx):
            acc[i] += part[:, j * D : (j + 1) * D]

    @pl.when(step == pl.num_programs(0) - 1)
    def _():
        def body(i, carry):
            dv_ref[i] = acc[i].T.astype(BF16)
            return carry

        lax.fori_loop(0, nb, body, 0)


def probs_call(glob, rand, qkg, nb, scale):
    half = nb // 2
    return pl.pallas_call(
        functools.partial(probs_kernel, nb, scale),
        grid=(half,),
        out_shape=[
            jax.ShapeDtypeStruct((nb, BLOCK, 8 * BLOCK), BF16),
            jax.ShapeDtypeStruct((nb, BLOCK, D), BF16),
        ],
        in_specs=[
            pl.BlockSpec(memory_space=pltpu.SMEM),
            pl.BlockSpec(memory_space=pltpu.SMEM),
            pl.BlockSpec((1, 2, BLOCK, D), lambda i: (i, 0, 0, 0)),
            pl.BlockSpec((half, 2, BLOCK, D), lambda i: (0, 1, 0, 0)),
            pl.BlockSpec((1, 2, BLOCK, D), lambda i: (i, 2, 0, 0)),
        ],
        out_specs=[
            pl.BlockSpec((2, BLOCK, 8 * BLOCK), lambda i: (i, 0, 0)),
            pl.BlockSpec((nb, BLOCK, D), lambda i: (0, 0, 0)),
        ],
        scratch_shapes=[pltpu.VMEM((nb, D, BLOCK), F32)],
        compiler_params=pltpu.CompilerParams(
            dimension_semantics=("arbitrary",), vmem_limit_bytes=32 * 1024 * 1024
        ),
        name="probs",
        cost_estimate=pl.CostEstimate(
            flops=4 * nb * 8 * BLOCK * BLOCK * D,
            bytes_accessed=12 * 1024 * 1024,
            transcendentals=nb * 8 * BLOCK * BLOCK,
        ),
    )(glob, rand, qkg, qkg, qkg)


def grads_kernel(nb, scale, glob_ref, rand_ref, q_ref, k_ref, g_ref, v_ref, p_ref, out_ref, acc):
    step = pl.program_id(0)
    per = q_ref.shape[1]

    @pl.when(step == 0)
    def _():
        acc[...] = jnp.zeros_like(acc)

    for u in range(per):
        b = step * per + u
        idx, _ = table_row(glob_ref, rand_ref, b, nb)
        vals = jnp.concatenate([v_ref[i // 2, i % 2] for i in idx], axis=0)
        keys = jnp.concatenate([k_ref[i // 2, i % 2] for i in idx], axis=0)
        dp = nt(g_ref[0, u], vals)
        p = p_ref[u]
        ps = [p[:, j * D : (j + 1) * D].astype(F32) for j in range(8)]
        ts = [ps[j] * dp[:, j * D : (j + 1) * D] for j in range(8)]
        delta = jnp.sum(functools.reduce(jnp.add, ts), axis=1, keepdims=True)
        ds = jnp.concatenate(
            [((t - x * delta) * scale).astype(BF16) for t, x in zip(ts, ps)], axis=1
        )
        dq = jnp.dot(ds, keys, preferred_element_type=F32)
        out_ref[step, u] = dq.astype(BF16)
        part = jnp.dot(q_ref[0, u].T, ds, preferred_element_type=F32)
        for j, i in enumerate(idx):
            acc[i] += part[:, j * D : (j + 1) * D]

    @pl.when(step == pl.num_programs(0) - 1)
    def _():
        def body(i, carry):
            out_ref[i // 2, 2 + i % 2] = acc[i].T.astype(BF16)
            return carry

        lax.fori_loop(0, nb, body, 0)


def grads_call(glob, rand, qkg, v, p, nb, scale):
    half = nb // 2
    return pl.pallas_call(
        functools.partial(grads_kernel, nb, scale),
        grid=(half,),
        out_shape=jax.ShapeDtypeStruct((half, 4, BLOCK, D), BF16),
        in_specs=[
            pl.BlockSpec(memory_space=pltpu.SMEM),
            pl.BlockSpec(memory_space=pltpu.SMEM),
            pl.BlockSpec((1, 2, BLOCK, D), lambda i: (i, 0, 0, 0)),
            pl.BlockSpec((half, 2, BLOCK, D), lambda i: (0, 1, 0, 0)),
            pl.BlockSpec((1, 2, BLOCK, D), lambda i: (i, 2, 0, 0)),
            pl.BlockSpec((half, 2, BLOCK, D), lambda i: (0, 0, 0, 0)),
            pl.BlockSpec((2, BLOCK, 8 * BLOCK), lambda i: (i, 0, 0)),
        ],
        out_specs=pl.BlockSpec((half, 4, BLOCK, D), lambda i: (0, 0, 0, 0)),
        scratch_shapes=[pltpu.VMEM((nb, D, BLOCK), F32)],
        compiler_params=pltpu.CompilerParams(
            dimension_semantics=("arbitrary",), vmem_limit_bytes=32 * 1024 * 1024
        ),
        name="grads",
        cost_estimate=pl.CostEstimate(
            flops=6 * nb * 8 * BLOCK * BLOCK * D,
            bytes_accessed=14 * 1024 * 1024,
            transcendentals=0,
        ),
    )(glob, rand, qkg, qkg, qkg, v, p)


def swap(array, axes):
    return lax.all_to_all(array, axes, split_axis=0, concat_axis=0, tiled=True)


def per_device(queries, keys, values, out_grad, layer_input, global_blocks, random_blocks):
    x = layer_input[0]
    local, features = x.shape
    n_ctx, n_dp = lax.axis_size(CTX), lax.axis_size(DP)
    nx, nz = lax.axis_size("x"), lax.axis_size(("zl", "core"))
    ny, nr = lax.axis_size("y"), lax.axis_size(("zh", "x"))
    doc = local * n_ctx
    nb = doc // BLOCK
    scale = 1.0 / math.sqrt(D)

    x_all = lax.all_gather(x, ("zl", "core"), axis=0, tiled=True)
    qkg, v_in = pack((queries, keys, out_grad), (values,))
    qkg = swap(qkg, CTX)
    qkg, v_in = lax.optimization_barrier((qkg, v_in))
    v_in = swap(v_in, CTX).reshape(n_ctx, 2, BLOCK, D)
    qkg = qkg.reshape(n_ctx, 6, BLOCK, D)
    probs, dv = probs_call(global_blocks, random_blocks, qkg, nb, scale)
    v_in, dv = lax.optimization_barrier((v_in, dv))
    dv_mid = swap(dv.reshape(nx, doc // nx, D), "x")
    qk_out = grads_call(global_blocks, random_blocks, qkg, v_in, probs, nb, scale)
    dv_mid, qk_out = lax.optimization_barrier((dv_mid, qk_out))
    qk_back = swap(qk_out.reshape(n_ctx, 2 * local, D), CTX)

    dv_cols = jnp.transpose(dv_mid, (1, 0, 2)).reshape(doc // nx, nx * D)
    w_part = lax.dot_general(
        x_all, dv_cols, (((0,), (0,)), ((), ())), preferred_element_type=F32
    ).astype(BF16)
    w_y = lax.psum_scatter(w_part, "y", scatter_dimension=0, tiled=True)
    last = ("zh", "x", "zl", "core")
    rows = features // (n_dp * n_ctx)
    w_all = swap(w_y.reshape(nr * nz, rows, nx * D), last)
    w_sum = jnp.sum(w_all.reshape(nr, nz, rows, nx, D).astype(F32), axis=0)
    w_out = jnp.transpose(w_sum, (1, 2, 0, 3)).reshape(rows, nx * nz * D)
    w_out = w_out * (1.0 / math.sqrt(doc * n_dp))

    dv_send = jnp.transpose(dv_mid.reshape(nx, nz, local, D), (1, 0, 2, 3))
    dv_back = swap(dv_send, ("zl", "core"))
    dv_out = jnp.transpose(dv_back, (2, 1, 0, 3)).reshape(local, n_ctx * D)
    dq, dk = unpack(qk_back, 2)
    return (dq, dk, dv_out[None], w_out)


def solution(mesh):
    fine = Mesh(mesh.devices.reshape(4, 2, 4, 2, 2), DP + CTX)
    tokens = P(DP, CTX, None)
    return jax.shard_map(
        per_device,
        mesh=fine,
        in_specs=(tokens,) * 5 + (P(DP, None), P(DP, None, None)),
        out_specs=(tokens, tokens, tokens, P(DP + CTX, None)),
        check_vma=False,
    )
```

```python
import functools
import math

import jax
import jax.numpy as jnp
from jax import lax
from jax.experimental import pallas as pl
from jax.experimental.pallas import tpu as pltpu
from jax.sharding import Mesh, PartitionSpec as P

D = 128
BLOCK = 128
F32 = jnp.float32
BF16 = jnp.bfloat16
LOG2E = 1.4426950408889634
DP = ("y", "zh")
CTX = ("x", "zl", "core")
NEG = float("-inf")


def hbm(array):
    return pltpu.with_memory_space_constraint(array, pltpu.HBM)


def pack_kernel(groups, *refs):
    count = sum(groups)
    ins, outs = refs[:count], refs[count : count + len(groups)]
    bufs, sems = refs[count + len(groups)], refs[count + len(groups) + 1]
    copies = [pltpu.make_async_copy(src.at[0], bufs.at[n], sems.at[n]) for n, src in enumerate(ins)]
    for c in copies:
        c.start()
    first = 0
    for out, size in zip(outs, groups):
        rows = bufs.shape[1]
        for n in range(size):
            copies[first + n].wait()
            for h in range(out.shape[0]):
                out[h, n * rows : (n + 1) * rows, :] = bufs[first + n, :, h * D : (h + 1) * D]
        first += size


def pack(*groups):
    flat = [a for group in groups for a in group]
    rows, cols = flat[0].shape[1:]
    heads = cols // D
    return pl.pallas_call(
        functools.partial(pack_kernel, tuple(len(group) for group in groups)),
        out_shape=[pltpu.HBM((heads, len(group) * rows, D), BF16) for group in groups],
        in_specs=[pl.BlockSpec(memory_space=pl.ANY)] * len(flat),
        out_specs=[pl.BlockSpec(memory_space=pltpu.VMEM)] * len(groups),
        scratch_shapes=[
            pltpu.VMEM((len(flat), rows, cols), BF16),
            pltpu.SemaphoreType.DMA((len(flat),)),
        ],
        compiler_params=pltpu.CompilerParams(vmem_limit_bytes=24 * 1024 * 1024),
        name="pack",
        cost_estimate=pl.CostEstimate(
            flops=0, bytes_accessed=4 * rows * cols * len(flat), transcendentals=0
        ),
    )(*[hbm(a) for a in flat])


def unpack_kernel(count, src, *outs):
    rows = outs[0].shape[1]
    for n, out in enumerate(outs):
        for h in range(src.shape[0]):
            out[0, :, h * D : (h + 1) * D] = src[h, n * rows : (n + 1) * rows, :]


def unpack(array, count):
    heads, rows = array.shape[0], array.shape[1] // count
    return pl.pallas_call(
        functools.partial(unpack_kernel, count),
        out_shape=[jax.ShapeDtypeStruct((1, rows, heads * D), BF16)] * count,
        in_specs=[pl.BlockSpec(memory_space=pltpu.VMEM)],
        out_specs=[pl.BlockSpec(memory_space=pltpu.VMEM)] * count,
        compiler_params=pltpu.CompilerParams(vmem_limit_bytes=24 * 1024 * 1024),
        name="unpack",
        cost_estimate=pl.CostEstimate(
            flops=0, bytes_accessed=4 * rows * heads * D * count, transcendentals=0
        ),
    )(array)


def table_row(glob_ref, rand_ref, b, nb):
    left, right = b - 1, b + 1
    g0, g1 = glob_ref[0, 0], glob_ref[0, 1]
    idx = [
        jnp.maximum(left, 0),
        b,
        jnp.minimum(right, nb - 1),
        g0,
        g1,
        rand_ref[0, b, 0],
        rand_ref[0, b, 1],
        rand_ref[0, b, 2],
    ]

    def bias(c):
        return jnp.where(c, 0.0, NEG).astype(F32)

    biases = [
        bias(left >= 0),
        None,
        bias(right < nb),
        bias(jnp.abs(g0 - b) > 1),
        bias(jnp.abs(g1 - b) > 1),
        None,
        None,
        None,
    ]
    return idx, biases


def nt(a, b):
    return lax.dot_general(a, b, (((1,), (1,)), ((), ())), preferred_element_type=F32)


def tn(a, b):
    return lax.dot_general(a, b, (((0,), (0,)), ((), ())), preferred_element_type=F32)


def diag(a, b):
    zero = jnp.zeros_like(a)
    return jnp.concatenate(
        [jnp.concatenate([a, zero], axis=1), jnp.concatenate([zero, b], axis=1)], axis=0
    )


def pick(ref, idx):
    return jnp.concatenate([ref[i // 2, i % 2] for i in idx], axis=0)


def tile(array, j, half):
    return array[j * D : (j + 1) * D, half * D : (half + 1) * D]


def add_tiles(acc, idx_pair, part):
    for j in range(8):
        for half, idx in enumerate(idx_pair):
            acc[idx[j]] += tile(part, j, half)


def probs_kernel(
    nb, nx, scale, glob_ref, rand_ref, me_ref, q_ref, k_ref, g_ref, p_ref, dv_ref, *rest
):
    parts, acc = rest[:-1], rest[-1]
    step = pl.program_id(0)
    pairs = q_ref.shape[0]

    @pl.when(step == 0)
    def _():
        acc[...] = jnp.zeros_like(acc)

    for u in range(pairs):
        b = (step * pairs + u) * 2
        rows = [table_row(glob_ref, rand_ref, b + half, nb) for half in range(2)]
        idx_pair = [row[0] for row in rows]
        keys = jnp.concatenate([pick(k_ref, idx) for idx in idx_pair], axis=1)
        s = nt(keys, diag(q_ref[u, 0], q_ref[u, 1]))
        ps = []
        for half, (_, biases) in enumerate(rows):
            tiles = [tile(s, j, half) for j in range(8)]
            tiles = [t if c is None else t + c for t, c in zip(tiles, biases)]
            top = jnp.max(functools.reduce(jnp.maximum, tiles), axis=0, keepdims=True)
            e = [jnp.exp2((t - top) * (scale * LOG2E)) for t in tiles]
            inv = 1.0 / jnp.sum(functools.reduce(jnp.add, e), axis=0, keepdims=True)
            ps.append(jnp.concatenate([(t * inv).astype(BF16) for t in e], axis=0))
        p = jnp.concatenate(ps, axis=1)
        p_ref[u] = p
        part = jnp.dot(p, diag(g_ref[u, 0], g_ref[u, 1]), preferred_element_type=F32)
        add_tiles(acc, idx_pair, part)

    @pl.when(step == pl.num_programs(0) - 1)
    def _():
        dv_ref[...] = acc[...].astype(BF16).reshape(dv_ref.shape)
        size = parts[0].shape[0]
        for n, part in enumerate(parts):
            part[...] = dv_ref[pl.ds(lax.rem(me_ref[0] + n, nx) * size, size)]


def probs_call(glob, rand, me, qkg, nb, nx, scale):
    half, pairs = nb // 2, 4
    return pl.pallas_call(
        functools.partial(probs_kernel, nb, nx, scale),
        grid=(half // pairs,),
        out_shape=[
            pltpu.HBM((half, 8 * BLOCK, 2 * BLOCK), BF16),
            pltpu.HBM((half, 2, BLOCK, D), BF16),
        ]
        + [pltpu.HBM((half // nx, 2, BLOCK, D), BF16)] * nx,
        in_specs=[pl.BlockSpec(memory_space=pltpu.SMEM)] * 3
        + [
            pl.BlockSpec((pairs, 2, BLOCK, D), lambda i: (i, 0, 0, 0)),
            pl.BlockSpec((half, 2, BLOCK, D), lambda i: (0, 1, 0, 0)),
            pl.BlockSpec((pairs, 2, BLOCK, D), lambda i: (i, 2, 0, 0)),
        ],
        out_specs=[
            pl.BlockSpec((pairs, 8 * BLOCK, 2 * BLOCK), lambda i: (i, 0, 0)),
            pl.BlockSpec((half, 2, BLOCK, D), lambda i: (0, 0, 0, 0)),
        ]
        + [pl.BlockSpec((half // nx, 2, BLOCK, D), lambda i: (0, 0, 0, 0))] * nx,
        scratch_shapes=[pltpu.VMEM((nb, BLOCK, D), F32)],
        compiler_params=pltpu.CompilerParams(
            dimension_semantics=("arbitrary",), vmem_limit_bytes=32 * 1024 * 1024
        ),
        name="probs",
        cost_estimate=pl.CostEstimate(
            flops=8 * nb * 8 * BLOCK * BLOCK * D,
            bytes_accessed=14 * 1024 * 1024,
            transcendentals=nb * 8 * BLOCK * BLOCK,
        ),
    )(glob, rand, me, qkg, qkg, qkg)


def grads_kernel(
    nb, scale, glob_ref, rand_ref, q_ref, k_ref, g_ref, v_ref, p_ref, dv_ref, out_ref, acc
):
    step = pl.program_id(0)
    pairs = q_ref.shape[0]

    @pl.when(step == 0)
    def _():
        acc[...] = jnp.zeros_like(acc)

    for u in range(pairs):
        b = (step * pairs + u) * 2
        idx_pair = [table_row(glob_ref, rand_ref, b + half, nb)[0] for half in range(2)]
        vals = jnp.concatenate([pick(v_ref, idx) for idx in idx_pair], axis=1)
        dp = nt(vals, diag(g_ref[u, 0], g_ref[u, 1]))
        both = []
        for half, idx in enumerate(idx_pair):
            ps = [tile(p_ref[u], j, half).astype(F32) for j in range(8)]
            ts = [ps[j] * tile(dp, j, half) for j in range(8)]
            delta = jnp.sum(functools.reduce(jnp.add, ts), axis=0, keepdims=True)
            ds = jnp.concatenate([(t - x * delta).astype(BF16) for t, x in zip(ts, ps)], axis=0)
            both.append(ds)
            dq = tn(ds, pick(k_ref, idx)) * scale
            out_ref[step * pairs + u, half] = dq.astype(BF16)
        ds = jnp.concatenate(both, axis=1)
        part = jnp.dot(ds, diag(q_ref[u, 0], q_ref[u, 1]), preferred_element_type=F32)
        add_tiles(acc, idx_pair, part)

    @pl.when(step == pl.num_programs(0) - 1)
    def _():
        out_ref[:, 2:4] = (acc[...] * scale).astype(BF16).reshape(nb // 2, 2, BLOCK, D)
        out_ref[:, 4:6] = dv_ref[...]


def grads_call(glob, rand, qkg, v, p, dv, nb, scale):
    half, pairs = nb // 2, 4
    return pl.pallas_call(
        functools.partial(grads_kernel, nb, scale),
        grid=(half // pairs,),
        out_shape=pltpu.HBM((half, 6, BLOCK, D), BF16),
        in_specs=[pl.BlockSpec(memory_space=pltpu.SMEM)] * 2
        + [
            pl.BlockSpec((pairs, 2, BLOCK, D), lambda i: (i, 0, 0, 0)),
            pl.BlockSpec((half, 2, BLOCK, D), lambda i: (0, 1, 0, 0)),
            pl.BlockSpec((pairs, 2, BLOCK, D), lambda i: (i, 2, 0, 0)),
            pl.BlockSpec((half, 2, BLOCK, D), lambda i: (0, 0, 0, 0)),
            pl.BlockSpec((pairs, 8 * BLOCK, 2 * BLOCK), lambda i: (i, 0, 0)),
            pl.BlockSpec((half, 2, BLOCK, D), lambda i: (0, 0, 0, 0)),
        ],
        out_specs=pl.BlockSpec((half, 6, BLOCK, D), lambda i: (0, 0, 0, 0)),
        scratch_shapes=[pltpu.VMEM((nb, BLOCK, D), F32)],
        compiler_params=pltpu.CompilerParams(
            dimension_semantics=("arbitrary",), vmem_limit_bytes=32 * 1024 * 1024
        ),
        name="grads",
        cost_estimate=pl.CostEstimate(
            flops=10 * nb * 8 * BLOCK * BLOCK * D,
            bytes_accessed=14 * 1024 * 1024,
            transcendentals=0,
        ),
    )(glob, rand, qkg, qkg, qkg, v, hbm(p), hbm(dv))


def weight_kernel(count, nx, nz, ny, me_ref, *refs):
    xs, parts, refs = refs[:count], refs[count : count + nx], refs[count + nx :]
    outs, cols = refs[:ny], refs[ny]
    rows = cols.shape[0] // nz
    step = pl.program_id(0)

    @pl.when(step == 0)
    def _():
        for n, part in enumerate(parts):
            head = pl.multiple_of(lax.rem(me_ref[0] + nx - n, nx) * D, D)
            for m in range(nz):
                first = pl.multiple_of((me_ref[1] ^ m) * rows, rows)
                cols[m * rows : (m + 1) * rows, pl.ds(head, D)] = part[pl.ds(first, rows), :]

    x = jnp.concatenate([ref[0] for ref in xs], axis=0)
    w = tn(x, cols[...]).astype(BF16)
    for n, out in enumerate(outs):

        @pl.when(step == n)
        def _():
            out[...] = w


def weight_call(me, xs, parts, nz, ny):
    nx, tokens = len(parts), parts[0].shape[0]
    features = xs[0].shape[2]
    size = features // ny
    grid_spec = pltpu.PrefetchScalarGridSpec(
        num_scalar_prefetch=1,
        grid=(ny,),
        in_specs=[
            pl.BlockSpec((1, x.shape[1], size), lambda i, me: (0, 0, lax.rem(me[2] + i, ny)))
            for x in xs
        ]
        + [pl.BlockSpec(parts[0].shape, lambda i, me: (0, 0))] * nx,
        out_specs=[pl.BlockSpec((size, nx * D), lambda i, me: (0, 0))] * ny,
        scratch_shapes=[pltpu.VMEM((tokens, nx * D), BF16)],
    )
    return pl.pallas_call(
        functools.partial(weight_kernel, len(xs), nx, nz, ny),
        grid_spec=grid_spec,
        out_shape=[pltpu.HBM((size, nx * D), BF16)] * ny,
        compiler_params=pltpu.CompilerParams(
            dimension_semantics=("arbitrary",), vmem_limit_bytes=24 * 1024 * 1024
        ),
        name="weight",
        cost_estimate=pl.CostEstimate(
            flops=2 * tokens * features * nx * D,
            bytes_accessed=7 * 1024 * 1024,
            transcendentals=0,
        ),
    )(me, *[hbm(x) for x in xs], *[hbm(part) for part in parts])


def add_kernel(*refs):
    total = refs[0][...].astype(F32)
    for ref in refs[1:-1]:
        total = total + ref[...].astype(F32)
    refs[-1][...] = total.astype(BF16)


def add_call(arrays):
    shape = arrays[0].shape
    return pl.pallas_call(
        add_kernel,
        out_shape=pltpu.HBM(shape, BF16),
        in_specs=[pl.BlockSpec(memory_space=pltpu.VMEM)] * len(arrays),
        out_specs=pl.BlockSpec(memory_space=pltpu.VMEM),
        name="add",
        cost_estimate=pl.CostEstimate(
            flops=arrays[0].size * 3, bytes_accessed=arrays[0].size * 10, transcendentals=0
        ),
    )(*arrays)


def sum_kernel(nz, nx, scale, in_ref, out_ref):
    for n in range(nz):
        total = in_ref[n].astype(F32)
        for r in range(1, in_ref.shape[0] // nz):
            total = total + in_ref[r * nz + n].astype(F32)
        total = total * scale
        for h in range(nx):
            c = (h * nz + n) * D
            out_ref[:, c : c + D] = total[:, h * D : (h + 1) * D]


def sum_call(array, nz, nx, scale):
    rows = array.shape[1]
    return pl.pallas_call(
        functools.partial(sum_kernel, nz, nx, scale),
        out_shape=jax.ShapeDtypeStruct((rows, nz * nx * D), F32),
        in_specs=[pl.BlockSpec(memory_space=pltpu.VMEM)],
        out_specs=pl.BlockSpec(memory_space=pltpu.VMEM),
        name="sum",
        cost_estimate=pl.CostEstimate(
            flops=array.size, bytes_accessed=2 * array.size, transcendentals=0
        ),
    )(array)


def swap(array, axes):
    return lax.all_to_all(array, axes, split_axis=0, concat_axis=0, tiled=True)


def shift(array, axis, n, size):
    return lax.ppermute(array, axis, [(i, (i + n) % size) for i in range(size)])


def per_device(queries, keys, values, out_grad, layer_input, global_blocks, random_blocks):
    local, features = layer_input.shape[1:]
    n_ctx, n_dp = lax.axis_size(CTX), lax.axis_size(DP)
    nx, ny, nz = lax.axis_size("x"), lax.axis_size("y"), lax.axis_size(("zl", "core"))
    nr = lax.axis_size(("zh", "x"))
    doc = local * n_ctx
    nb = doc // BLOCK
    scale = 1.0 / math.sqrt(D)
    me = [lax.axis_index("x"), lax.axis_index(("zl", "core")), lax.axis_index("y")]
    me = jnp.stack(me).astype(jnp.int32)

    qkg, v_in = pack((queries, keys, out_grad), (values,))
    qkg = swap(qkg, CTX)
    qkg, v_in, x_own = lax.optimization_barrier((qkg, v_in, layer_input))
    v_in = swap(v_in, CTX).reshape(n_ctx, 2, BLOCK, D)
    qkg = qkg.reshape(n_ctx, 6, BLOCK, D)
    probs, dv, *parts = probs_call(global_blocks, random_blocks, me, qkg, nb, nx, scale)
    parts = [part.reshape(doc // nx, D) for part in parts]
    cut = local * 3 // 8
    x_core = shift(x_own, "core", 1, 2)
    x_zl = [shift(x_own[:, :cut], "zl", 1, 2)]
    v_in, x_own, x_core, x_zl[0], *parts = lax.optimization_barrier(
        (v_in, x_own, x_core, x_zl[0], *parts)
    )
    parts = parts[:1] + [shift(parts[n], "x", n, nx) for n in range(1, nx)]
    x_zl.append(shift(x_own[:, cut:], "zl", 1, 2))
    x_both = [shift(x_zl[0], "core", 1, 2)]
    qkv = grads_call(global_blocks, random_blocks, qkg, v_in, probs, dv, nb, scale)
    qkv, x_zl[1], x_both[0], *parts = lax.optimization_barrier((qkv, x_zl[1], x_both[0], *parts))
    back = swap(qkv.reshape(n_ctx, 3 * local, D), CTX)
    x_both.append(shift(x_zl[1], "core", 1, 2))
    xs = [x_own, x_core, *x_zl, *x_both]
    w_parts = weight_call(me, xs, parts, nz, ny)
    w_y = add_call([w_parts[0]] + [shift(w_parts[n], "y", n, ny) for n in range(1, ny)])

    rows = features // (n_dp * n_ctx)
    w_y, back = lax.optimization_barrier((w_y, back))
    w_all = swap(w_y.reshape(nr * nz, rows, nx * D), ("zh", "x", "zl", "core"))
    w_out = sum_call(w_all, nz, nx, 1.0 / math.sqrt(doc * n_dp))
    dq, dk, dv_out = unpack(back, 3)
    return (dq, dk, dv_out, w_out)


def solution(mesh):
    fine = Mesh(mesh.devices.reshape(4, 2, 4, 2, 2), DP + CTX)
    tokens = P(DP, CTX, None)
    return jax.shard_map(
        per_device,
        mesh=fine,
        in_specs=(tokens,) * 5 + (P(DP, None), P(DP, None, None)),
        out_specs=(tokens, tokens, tokens, P(DP + CTX, None)),
        check_vma=False,
    )
```

```python
import functools
import math

import jax
import jax.numpy as jnp
from jax import lax
from jax.experimental import pallas as pl
from jax.experimental.pallas import tpu as pltpu
from jax.sharding import Mesh, PartitionSpec as P

D = 128
BLOCK = 128
F32 = jnp.float32
BF16 = jnp.bfloat16
LOG2E = 1.4426950408889634
DP = ("y", "zh")
CTX = ("x", "zl", "core")
NEG = float("-inf")


def hbm(array):
    return pltpu.with_memory_space_constraint(array, pltpu.HBM)


def pack_kernel(pieces, *refs):
    ins, (out, bufs, sems) = refs[:-3], refs[-3:]
    count, rows = bufs.shape[:2]
    size = rows // pieces
    copies = {}
    for m in range(pieces):
        for n, src in enumerate(ins):
            at = pl.ds(m * size, size)
            copies[m, n] = pltpu.make_async_copy(src.at[0, at], bufs.at[n, at], sems.at[m, n])
            copies[m, n].start()
    for m in range(pieces):
        for n in range(count):
            copies[m, n].wait()
            first = n * rows + m * size
            for h in range(out.shape[0]):
                out[h, first : first + size, :] = bufs[
                    n, m * size : (m + 1) * size, h * D : (h + 1) * D
                ]


def pack(*arrays):
    rows, cols = arrays[0].shape[1:]
    heads, count, pieces = cols // D, len(arrays), 4
    return pl.pallas_call(
        functools.partial(pack_kernel, pieces),
        out_shape=jax.ShapeDtypeStruct((heads, count * rows, D), BF16),
        in_specs=[pl.BlockSpec(memory_space=pl.ANY)] * count,
        out_specs=pl.BlockSpec(memory_space=pltpu.VMEM),
        scratch_shapes=[
            pltpu.VMEM((count, rows, cols), BF16),
            pltpu.SemaphoreType.DMA((pieces, count)),
        ],
        compiler_params=pltpu.CompilerParams(vmem_limit_bytes=24 * 1024 * 1024),
        name="pack",
        cost_estimate=pl.CostEstimate(
            flops=0, bytes_accessed=4 * rows * cols * count, transcendentals=0
        ),
    )(*[hbm(a) for a in arrays])


def unpack_kernel(count, src, *outs):
    rows = outs[0].shape[1]
    for n, out in enumerate(outs):
        for h in range(src.shape[0]):
            out[0, :, h * D : (h + 1) * D] = src[h, n * rows : (n + 1) * rows, :]


def unpack(array, count):
    heads, rows = array.shape[0], array.shape[1] // count
    return pl.pallas_call(
        functools.partial(unpack_kernel, count),
        out_shape=[jax.ShapeDtypeStruct((1, rows, heads * D), BF16)] * count,
        in_specs=[pl.BlockSpec(memory_space=pltpu.VMEM)],
        out_specs=[pl.BlockSpec(memory_space=pltpu.VMEM)] * count,
        compiler_params=pltpu.CompilerParams(vmem_limit_bytes=24 * 1024 * 1024),
        name="unpack",
        cost_estimate=pl.CostEstimate(
            flops=0, bytes_accessed=4 * rows * heads * D * count, transcendentals=0
        ),
    )(array)


def table_row(glob_ref, rand_ref, b, nb):
    left, right = b - 1, b + 1
    g0, g1 = glob_ref[0, 0], glob_ref[0, 1]
    idx = [
        jnp.maximum(left, 0),
        b,
        jnp.minimum(right, nb - 1),
        g0,
        g1,
        rand_ref[0, b, 0],
        rand_ref[0, b, 1],
        rand_ref[0, b, 2],
    ]

    def bias(c):
        return jnp.where(c, 0.0, NEG).astype(F32)

    biases = [
        bias(left >= 0),
        None,
        bias(right < nb),
        bias(jnp.abs(g0 - b) > 1),
        bias(jnp.abs(g1 - b) > 1),
        None,
        None,
        None,
    ]
    return idx, biases


def nt(a, b):
    return lax.dot_general(a, b, (((1,), (1,)), ((), ())), preferred_element_type=F32)


def tn(a, b):
    return lax.dot_general(a, b, (((0,), (0,)), ((), ())), preferred_element_type=F32)


def diag(a, b):
    zero = jnp.zeros_like(a)
    return jnp.concatenate(
        [jnp.concatenate([a, zero], axis=1), jnp.concatenate([zero, b], axis=1)], axis=0
    )


def pick(ref, idx, kind):
    return jnp.concatenate([ref[i // 2, 2 * kind + i % 2] for i in idx], axis=0)


def two(ref, u, kind):
    return diag(ref[u, 2 * kind], ref[u, 2 * kind + 1])


def tile(array, j, half):
    return array[j * D : (j + 1) * D, half * D : (half + 1) * D]


def add_tiles(acc, idx_pair, part):
    for j in range(8):
        for half, idx in enumerate(idx_pair):
            acc[idx[j]] += tile(part, j, half)


Q, K, G, V = 0, 1, 2, 3
DQ, DK, DV = 0, 1, 2
UNROLL = 8
LOADS = 4


def probs_kernel(nx, scale, glob_ref, rand_ref, me_ref, in_hbm, p_ref, dv_ref, *rest):
    parts, (acc, buf, sems) = rest[:-3], rest[-3:]
    half_nb, nb = buf.shape[0], acc.shape[0]
    copies = []
    for kind in (K, Q, G):
        at = pl.ds(2 * kind, 2)
        for piece in range(LOADS):
            size = half_nb // LOADS
            rows = pl.ds(piece * size, size)
            copies.append(
                pltpu.make_async_copy(
                    in_hbm.at[rows, at], buf.at[rows, at], sems.at[kind * LOADS + piece]
                )
            )
            copies[-1].start()
    acc[...] = jnp.zeros_like(acc)
    for copy in copies:
        copy.wait()
    in_ref = buf

    def pair(u):
        rows = [table_row(glob_ref, rand_ref, 2 * u + half, nb) for half in range(2)]
        idx_pair = [row[0] for row in rows]
        keys = jnp.concatenate([pick(in_ref, idx, K) for idx in idx_pair], axis=1)
        s = nt(keys, two(in_ref, u, Q))
        ps = []
        for half, (_, biases) in enumerate(rows):
            tiles = [tile(s, j, half) for j in range(8)]
            tiles = [t if c is None else t + c for t, c in zip(tiles, biases)]
            top = jnp.max(functools.reduce(jnp.maximum, tiles), axis=0, keepdims=True)
            e = [jnp.exp2((t - top) * (scale * LOG2E)) for t in tiles]
            inv = 1.0 / jnp.sum(functools.reduce(jnp.add, e), axis=0, keepdims=True)
            ps.append(jnp.concatenate([(t * inv).astype(BF16) for t in e], axis=0))
        p = jnp.concatenate(ps, axis=1)
        p_ref[u] = p
        part = jnp.dot(p, two(in_ref, u, G), preferred_element_type=F32)
        add_tiles(acc, idx_pair, part)

    @pl.loop(0, half_nb // UNROLL)
    def _(step):
        for u in range(UNROLL):
            pair(step * UNROLL + u)

    dv_ref[...] = acc[...].astype(BF16).reshape(dv_ref.shape)
    size = parts[0].shape[0]
    for n, part in enumerate(parts):
        part[...] = dv_ref[pl.ds(lax.rem(me_ref[0] + n, nx) * size, size)]


def probs_call(glob, rand, me, qkgv, nx, scale):
    half = qkgv.shape[0]
    smem, vmem = pl.BlockSpec(memory_space=pltpu.SMEM), pl.BlockSpec(memory_space=pltpu.VMEM)
    return pl.pallas_call(
        functools.partial(probs_kernel, nx, scale),
        out_shape=[
            jax.ShapeDtypeStruct((half, 8 * BLOCK, 2 * BLOCK), BF16),
            jax.ShapeDtypeStruct((half, 2, BLOCK, D), BF16),
        ]
        + [pltpu.HBM((half // nx, 2, BLOCK, D), BF16)] * nx,
        in_specs=[smem, smem, smem, pl.BlockSpec(memory_space=pl.ANY)],
        out_specs=[vmem] * (2 + nx),
        scratch_shapes=[
            pltpu.VMEM((2 * half, BLOCK, D), F32),
            pltpu.VMEM((half, 6, BLOCK, D), BF16),
            pltpu.SemaphoreType.DMA((3 * LOADS,)),
        ],
        compiler_params=pltpu.CompilerParams(vmem_limit_bytes=24 * 1024 * 1024),
        name="probs",
        cost_estimate=pl.CostEstimate(
            flops=16 * half * 8 * BLOCK * BLOCK * D,
            bytes_accessed=14 * 1024 * 1024,
            transcendentals=2 * half * 8 * BLOCK * BLOCK,
        ),
    )(glob, rand, me, hbm(qkgv))


def grads_kernel(scale, glob_ref, rand_ref, in_ref, p_ref, dv_ref, out_ref, acc):
    half_nb, nb = in_ref.shape[0], acc.shape[0]
    acc[...] = jnp.zeros_like(acc)
    def pair(u):
        idx_pair = [table_row(glob_ref, rand_ref, 2 * u + half, nb)[0] for half in range(2)]
        vals = jnp.concatenate([pick(in_ref, idx, V) for idx in idx_pair], axis=1)
        dp = nt(vals, two(in_ref, u, G))
        both = []
        for half, idx in enumerate(idx_pair):
            ps = [tile(p_ref[u], j, half).astype(F32) for j in range(8)]
            ts = [ps[j] * tile(dp, j, half) for j in range(8)]
            delta = jnp.sum(functools.reduce(jnp.add, ts), axis=0, keepdims=True)
            ds = jnp.concatenate([(t - x * delta).astype(BF16) for t, x in zip(ts, ps)], axis=0)
            both.append(ds)
            out_ref[u, 2 * DQ + half] = (tn(ds, pick(in_ref, idx, K)) * scale).astype(BF16)
        ds = jnp.concatenate(both, axis=1)
        part = jnp.dot(ds, two(in_ref, u, Q), preferred_element_type=F32)
        add_tiles(acc, idx_pair, part)

    @pl.loop(0, half_nb // UNROLL)
    def _(step):
        for u in range(UNROLL):
            pair(step * UNROLL + u)

    out_ref[:, 2 * DK : 2 * DK + 2] = (acc[...] * scale).astype(BF16).reshape(dv_ref.shape)
    out_ref[:, 2 * DV : 2 * DV + 2] = dv_ref[...]


def grads_call(glob, rand, qkgv, p, dv, scale):
    half = qkgv.shape[0]
    smem, vmem = pl.BlockSpec(memory_space=pltpu.SMEM), pl.BlockSpec(memory_space=pltpu.VMEM)
    return pl.pallas_call(
        functools.partial(grads_kernel, scale),
        out_shape=pltpu.HBM((half, 6, BLOCK, D), BF16),
        in_specs=[smem, smem, vmem, vmem, vmem],
        out_specs=vmem,
        scratch_shapes=[pltpu.VMEM((2 * half, BLOCK, D), F32)],
        compiler_params=pltpu.CompilerParams(vmem_limit_bytes=24 * 1024 * 1024),
        name="grads",
        cost_estimate=pl.CostEstimate(
            flops=20 * half * 8 * BLOCK * BLOCK * D,
            bytes_accessed=14 * 1024 * 1024,
            transcendentals=0,
        ),
    )(glob, rand, qkgv, p, dv)


def weight_kernel(count, nx, nz, ny, me_ref, *refs):
    xs, parts, refs = refs[:count], refs[count : count + nx], refs[count + nx :]
    outs, (x_buf, cols, bufs, in_sems, x_sems, out_sems) = refs[:ny], refs[ny:]
    rows, size = cols.shape[0] // nz, bufs.shape[1]
    loads = []
    for n, part in enumerate(parts):
        head = pl.multiple_of(lax.rem(me_ref[0] + nx - n, nx) * D, D)
        for m in range(nz):
            first = pl.multiple_of((me_ref[1] ^ m) * rows, rows)
            loads.append(
                pltpu.make_async_copy(
                    part.at[pl.ds(first, rows)],
                    cols.at[pl.ds(m * rows, rows), pl.ds(head, D)],
                    in_sems.at[n * nz + m],
                )
            )
            loads[-1].start()
    x_loads = []
    for n in range(ny):
        at = pl.ds(pl.multiple_of(lax.rem(me_ref[2] + n, ny) * size, size), size)
        for m, x in enumerate(xs):
            load = pltpu.make_async_copy(
                x.at[0, :, at], x_buf.at[n, pl.ds(m * rows, rows)], x_sems.at[n * count + m]
            )
            load.start()
            x_loads.append(load)
    for load in loads:
        load.wait()
    stores = []
    for n, out in enumerate(outs):
        for load in x_loads[n * count : (n + 1) * count]:
            load.wait()
        bufs[n] = tn(x_buf[n], cols[...]).astype(BF16)
        stores.append(pltpu.make_async_copy(bufs.at[n], out, out_sems.at[n]))
        stores[n].start()
    for store in stores:
        store.wait()


def weight_call(me, xs, parts, nz, ny):
    nx, tokens = len(parts), parts[0].shape[0]
    features = xs[0].shape[2]
    size = features // ny
    smem, hbm_spec = pl.BlockSpec(memory_space=pltpu.SMEM), pl.BlockSpec(memory_space=pl.ANY)
    return pl.pallas_call(
        functools.partial(weight_kernel, len(xs), nx, nz, ny),
        out_shape=[pltpu.HBM((size, nx * D), BF16)] * ny,
        in_specs=[smem] + [hbm_spec] * (len(xs) + nx),
        out_specs=[hbm_spec] * ny,
        scratch_shapes=[
            pltpu.VMEM((ny, tokens, size), BF16),
            pltpu.VMEM((tokens, nx * D), BF16),
            pltpu.VMEM((ny, size, nx * D), BF16),
            pltpu.SemaphoreType.DMA((nx * nz,)),
            pltpu.SemaphoreType.DMA((ny * len(xs),)),
            pltpu.SemaphoreType.DMA((ny,)),
        ],
        compiler_params=pltpu.CompilerParams(vmem_limit_bytes=24 * 1024 * 1024),
        name="weight",
        cost_estimate=pl.CostEstimate(
            flops=2 * tokens * features * nx * D,
            bytes_accessed=7 * 1024 * 1024,
            transcendentals=0,
        ),
    )(me, *[hbm(x) for x in xs], *[hbm(part) for part in parts])


def sum_kernel(nz, nx, scale, in_ref, out_ref):
    for n in range(nz):
        total = in_ref[n].astype(F32)
        for r in range(1, in_ref.shape[0] // nz):
            total = total + in_ref[r * nz + n].astype(F32)
        total = total * scale
        for h in range(nx):
            c = (h * nz + n) * D
            out_ref[:, c : c + D] = total[:, h * D : (h + 1) * D]


def sum_call(array, nz, nx, scale):
    rows = array.shape[1]
    return pl.pallas_call(
        functools.partial(sum_kernel, nz, nx, scale),
        out_shape=jax.ShapeDtypeStruct((rows, nz * nx * D), F32),
        in_specs=[pl.BlockSpec(memory_space=pltpu.VMEM)],
        out_specs=pl.BlockSpec(memory_space=pltpu.VMEM),
        name="sum",
        cost_estimate=pl.CostEstimate(
            flops=array.size, bytes_accessed=2 * array.size, transcendentals=0
        ),
    )(array)


def swap(array, axes):
    return lax.all_to_all(array, axes, split_axis=0, concat_axis=0, tiled=True)


def shift(array, axis, n, size):
    return lax.ppermute(array, axis, [(i, (i + n) % size) for i in range(size)])


def per_device(queries, keys, values, out_grad, layer_input, global_blocks, random_blocks):
    local, features = layer_input.shape[1:]
    n_ctx, n_dp = lax.axis_size(CTX), lax.axis_size(DP)
    nx, ny, nz = lax.axis_size("x"), lax.axis_size("y"), lax.axis_size(("zl", "core"))
    nr = lax.axis_size(("zh", "x"))
    doc = local * n_ctx
    nb = doc // BLOCK
    scale = 1.0 / math.sqrt(D)
    me = [lax.axis_index("x"), lax.axis_index(("zl", "core")), lax.axis_index("y")]
    me = jnp.stack(me).astype(jnp.int32)

    qkgv = swap(pack(queries, keys, out_grad, values), CTX)
    qkgv, x_own = lax.optimization_barrier((qkgv, layer_input))
    qkgv = qkgv.reshape(n_ctx, 8, BLOCK, D)
    x_zl = shift(x_own, "zl", 1, 2)
    x_core = shift(x_own, "core", 1, 2)
    probs, dv, *parts = probs_call(global_blocks, random_blocks, me, qkgv, nx, scale)
    parts = [part.reshape(doc // nx, D) for part in parts]
    parts = parts[:1] + [shift(parts[n], "x", n, nx) for n in range(1, nx)]
    qkv = grads_call(global_blocks, random_blocks, qkgv, probs, dv, scale)
    qkv, x_zl, x_core, *parts = lax.optimization_barrier((qkv, x_zl, x_core, *parts))
    back = swap(qkv.reshape(n_ctx, 3 * local, D), CTX)
    xs = [x_own, x_core, x_zl, shift(x_zl, "core", 1, 2)]
    w_parts = weight_call(me, xs, parts, nz, ny)
    w_parts = [w_parts[0]] + [shift(w_parts[n], "y", n, ny) for n in range(1, ny)]
    w_y = sum(part.astype(F32) for part in w_parts).astype(BF16)

    rows = features // (n_dp * n_ctx)
    w_y, back = lax.optimization_barrier((w_y, back))
    w_all = swap(w_y.reshape(nr * nz, rows, nx * D), ("zh", "x", "zl", "core"))
    w_out = sum_call(w_all, nz, nx, 1.0 / math.sqrt(doc * n_dp))
    dq, dk, dv_out = unpack(back, 3)
    return (dq, dk, dv_out, w_out)


def solution(mesh):
    fine = Mesh(mesh.devices.reshape(4, 2, 4, 2, 2), DP + CTX)
    tokens = P(DP, CTX, None)
    return jax.shard_map(
        per_device,
        mesh=fine,
        in_specs=(tokens,) * 5 + (P(DP, None), P(DP, None, None)),
        out_specs=(tokens, tokens, tokens, P(DP + CTX, None)),
        check_vma=False,
    )
```

```python
import functools
import math

import jax
import jax.numpy as jnp
from jax import lax
from jax.experimental import pallas as pl
from jax.experimental.pallas import tpu as pltpu
from jax.sharding import Mesh, PartitionSpec as P

D = 128
BLOCK = 128
F32 = jnp.float32
BF16 = jnp.bfloat16
LOG2E = 1.4426950408889634
DP = ("y", "zh")
CTX = ("x", "zl", "core")
NEG = float("-inf")


def vmem_pin(array):
    return pltpu.with_memory_space_constraint(array, pltpu.VMEM)


def hbm(array):
    return pltpu.with_memory_space_constraint(array, pltpu.HBM)


def pack_kernel(pieces, first_count, *refs):
    ins, (out, late_hbm, bufs, late, sems, late_sem) = refs[:-6], refs[-6:]
    count, rows = bufs.shape[:2]
    size = rows // pieces
    order = list(range(first_count, count)) + list(range(first_count))
    copies = {}
    for n in order:
        for m in range(pieces):
            at = pl.ds(m * size, size)
            copies[n, m] = pltpu.make_async_copy(ins[n].at[0, at], bufs.at[n, at], sems.at[n, m])
            copies[n, m].start()
    leave = pltpu.make_async_copy(late, late_hbm, late_sem)
    for n in order:
        to, i = (late, n - first_count) if n >= first_count else (out, n)
        for m in range(pieces):
            copies[n, m].wait()
            first = i * rows + m * size
            for h in range(out.shape[0]):
                to[h, first : first + size, :] = bufs[
                    n, m * size : (m + 1) * size, h * D : (h + 1) * D
                ]
        if n == count - 1:
            leave.start()
    leave.wait()


def pack(now, later):
    arrays = [*now, *later]
    rows, cols = arrays[0].shape[1:]
    heads, count, pieces = cols // D, len(arrays), 4
    late_shape = (heads, len(later) * rows, D)
    any_spec = pl.BlockSpec(memory_space=pl.ANY)
    return pl.pallas_call(
        functools.partial(pack_kernel, pieces, len(now)),
        out_shape=[
            jax.ShapeDtypeStruct((heads, len(now) * rows, D), BF16),
            pltpu.HBM(late_shape, BF16),
        ],
        in_specs=[any_spec] * count,
        out_specs=[pl.BlockSpec(memory_space=pltpu.VMEM), any_spec],
        scratch_shapes=[
            pltpu.VMEM((count, rows, cols), BF16),
            pltpu.VMEM(late_shape, BF16),
            pltpu.SemaphoreType.DMA((count, pieces)),
            pltpu.SemaphoreType.DMA,
        ],
        compiler_params=pltpu.CompilerParams(vmem_limit_bytes=24 * 1024 * 1024),
        name="pack",
        cost_estimate=pl.CostEstimate(
            flops=0, bytes_accessed=4 * rows * cols * count, transcendentals=0
        ),
    )(*[hbm(a) for a in arrays])


def unpack_kernel(count, src, *outs):
    rows = outs[0].shape[1]
    for n, out in enumerate(outs):
        for h in range(src.shape[0]):
            out[0, :, h * D : (h + 1) * D] = src[h, n * rows : (n + 1) * rows, :]


def unpack(array, count):
    heads, rows = array.shape[0], array.shape[1] // count
    return pl.pallas_call(
        functools.partial(unpack_kernel, count),
        out_shape=[jax.ShapeDtypeStruct((1, rows, heads * D), BF16)] * count,
        in_specs=[pl.BlockSpec(memory_space=pltpu.VMEM)],
        out_specs=[pl.BlockSpec(memory_space=pltpu.VMEM)] * count,
        compiler_params=pltpu.CompilerParams(vmem_limit_bytes=24 * 1024 * 1024),
        name="unpack",
        cost_estimate=pl.CostEstimate(
            flops=0, bytes_accessed=4 * rows * heads * D * count, transcendentals=0
        ),
    )(array)


def table_row(glob_ref, rand_ref, b, nb):
    left, right = b - 1, b + 1
    g0, g1 = glob_ref[0, 0], glob_ref[0, 1]
    idx = [
        jnp.maximum(left, 0),
        b,
        jnp.minimum(right, nb - 1),
        g0,
        g1,
        rand_ref[0, b, 0],
        rand_ref[0, b, 1],
        rand_ref[0, b, 2],
    ]

    def bias(c):
        return jnp.where(c, 0.0, NEG).astype(F32)

    biases = [
        bias(left >= 0),
        None,
        bias(right < nb),
        bias(jnp.abs(g0 - b) > 1),
        bias(jnp.abs(g1 - b) > 1),
        None,
        None,
        None,
    ]
    return idx, biases


def nt(a, b):
    return lax.dot_general(a, b, (((1,), (1,)), ((), ())), preferred_element_type=F32)


def tn(a, b):
    return lax.dot_general(a, b, (((0,), (0,)), ((), ())), preferred_element_type=F32)


def diag(a, b):
    zero = jnp.zeros_like(a)
    return jnp.concatenate(
        [jnp.concatenate([a, zero], axis=1), jnp.concatenate([zero, b], axis=1)], axis=0
    )


def pick(ref, idx, kind):
    return jnp.concatenate([ref[i // 2, 2 * kind + i % 2] for i in idx], axis=0)


def two(ref, u, kind):
    return diag(ref[u, 2 * kind], ref[u, 2 * kind + 1])


def tile(array, j, half):
    return array[j * D : (j + 1) * D, half * D : (half + 1) * D]


def add_tiles(acc, idx_pair, part):
    for j in range(8):
        for half, idx in enumerate(idx_pair):
            acc[idx[j]] += tile(part, j, half)


Q, K, G = 0, 1, 2
DQ, DK, DV = 0, 1, 2
LOADS = 4


def probs_kernel(nx, scale, glob_ref, rand_ref, me_ref, in_hbm, p_hbm, dv_ref, *rest):
    parts, (acc, buf, p_ref, sems, p_sems) = rest[:-5], rest[-5:]
    half_nb, nb = buf.shape[0], acc.shape[0]
    copies = []
    for kind in (K, Q, G):
        at = pl.ds(2 * kind, 2)
        for piece in range(LOADS):
            size = half_nb // LOADS
            rows = pl.ds(piece * size, size)
            copies.append(
                pltpu.make_async_copy(
                    in_hbm.at[rows, at], buf.at[rows, at], sems.at[kind * LOADS + piece]
                )
            )
            copies[-1].start()
    acc[...] = jnp.zeros_like(acc)
    for copy in copies:
        copy.wait()
    in_ref = buf

    def store(u):
        return pltpu.make_async_copy(p_ref.at[u], p_hbm.at[u], p_sems.at[u])

    def pair(u):
        rows = [table_row(glob_ref, rand_ref, 2 * u + half, nb) for half in range(2)]
        idx_pair = [row[0] for row in rows]
        keys = jnp.concatenate([pick(in_ref, idx, K) for idx in idx_pair], axis=1)
        s = nt(keys, two(in_ref, u, Q))
        ps = []
        for half, (_, biases) in enumerate(rows):
            tiles = [tile(s, j, half) for j in range(8)]
            tiles = [t if c is None else t + c for t, c in zip(tiles, biases)]
            top = jnp.max(functools.reduce(jnp.maximum, tiles), axis=0, keepdims=True)
            e = [jnp.exp2((t - top) * (scale * LOG2E)) for t in tiles]
            inv = 1.0 / jnp.sum(functools.reduce(jnp.add, e), axis=0, keepdims=True)
            ps.append(jnp.concatenate([(t * inv).astype(BF16) for t in e], axis=0))
        p = jnp.concatenate(ps, axis=1)
        p_ref[u] = p
        store(u).start()
        part = jnp.dot(p, two(in_ref, u, G), preferred_element_type=F32)
        add_tiles(acc, idx_pair, part)

    for u in range(half_nb):
        pair(u)
    dv_ref[...] = acc[...].astype(BF16).reshape(dv_ref.shape)
    size = parts[0].shape[0]
    for n, part in enumerate(parts):
        part[...] = dv_ref[pl.ds(lax.rem(me_ref[0] + n, nx) * size, size)]
    for u in range(half_nb):
        store(u).wait()


def probs_call(glob, rand, me, qkg, nx, scale):
    half = qkg.shape[0]
    smem, vmem = pl.BlockSpec(memory_space=pltpu.SMEM), pl.BlockSpec(memory_space=pltpu.VMEM)
    return pl.pallas_call(
        functools.partial(probs_kernel, nx, scale),
        out_shape=[
            pltpu.HBM((half, 8 * BLOCK, 2 * BLOCK), BF16),
            pltpu.HBM((half, 2, BLOCK, D), BF16),
        ]
        + [pltpu.HBM((half // nx, 2, BLOCK, D), BF16)] * nx,
        in_specs=[smem, smem, smem, pl.BlockSpec(memory_space=pl.ANY)],
        out_specs=[pl.BlockSpec(memory_space=pl.ANY)] + [vmem] * (1 + nx),
        scratch_shapes=[
            pltpu.VMEM((2 * half, BLOCK, D), F32),
            pltpu.VMEM((half, 6, BLOCK, D), BF16),
            pltpu.VMEM((half, 8 * BLOCK, 2 * BLOCK), BF16),
            pltpu.SemaphoreType.DMA((3 * LOADS,)),
            pltpu.SemaphoreType.DMA((half,)),
        ],
        compiler_params=pltpu.CompilerParams(vmem_limit_bytes=32 * 1024 * 1024),
        name="probs",
        cost_estimate=pl.CostEstimate(
            flops=16 * half * 8 * BLOCK * BLOCK * D,
            bytes_accessed=14 * 1024 * 1024,
            transcendentals=2 * half * 8 * BLOCK * BLOCK,
        ),
    )(glob, rand, me, hbm(qkg))


def grads_kernel(scale, glob_ref, rand_ref, in_ref, v_ref, p_hbm, dv_hbm, out_ref, *rest):
    acc, p_ref, sems = rest
    half_nb, nb = in_ref.shape[0], acc.shape[0]

    def load(u):
        return pltpu.make_async_copy(p_hbm.at[u], p_ref.at[u], sems.at[u])

    for u in range(half_nb):
        load(u).start()
    dv_load = pltpu.make_async_copy(dv_hbm, out_ref.at[:, pl.ds(2 * DV, 2)], sems.at[half_nb])
    dv_load.start()
    acc[...] = jnp.zeros_like(acc)
    def pair(u):
        idx_pair = [table_row(glob_ref, rand_ref, 2 * u + half, nb)[0] for half in range(2)]
        vals = jnp.concatenate([pick(v_ref, idx, 0) for idx in idx_pair], axis=1)
        dp = nt(vals, two(in_ref, u, G))
        both = []
        for half, idx in enumerate(idx_pair):
            ps = [tile(p_ref[u], j, half).astype(F32) for j in range(8)]
            ts = [ps[j] * tile(dp, j, half) for j in range(8)]
            delta = jnp.sum(functools.reduce(jnp.add, ts), axis=0, keepdims=True)
            ds = jnp.concatenate([(t - x * delta).astype(BF16) for t, x in zip(ts, ps)], axis=0)
            both.append(ds)
            out_ref[u, 2 * DQ + half] = (tn(ds, pick(in_ref, idx, K)) * scale).astype(BF16)
        ds = jnp.concatenate(both, axis=1)
        part = jnp.dot(ds, two(in_ref, u, Q), preferred_element_type=F32)
        add_tiles(acc, idx_pair, part)

    quarter = half_nb // 4

    def batch(first, size):
        for u in range(size):
            load(first + u).wait()
        for u in range(size):
            pair(first + u)

    @pl.loop(0, 2)
    def _(step):
        batch(step * quarter, quarter)

    batch(2 * quarter, 2 * quarter)
    out_ref[:, 2 * DK : 2 * DK + 2] = (acc[...] * scale).astype(BF16).reshape(dv_hbm.shape)
    dv_load.wait()


def grads_call(glob, rand, qkg, v, p, dv, scale):
    half = qkg.shape[0]
    smem, vmem = pl.BlockSpec(memory_space=pltpu.SMEM), pl.BlockSpec(memory_space=pltpu.VMEM)
    return pl.pallas_call(
        functools.partial(grads_kernel, scale),
        out_shape=pltpu.HBM((half, 6, BLOCK, D), BF16),
        in_specs=[smem, smem, vmem, vmem] + [pl.BlockSpec(memory_space=pl.ANY)] * 2,
        out_specs=vmem,
        scratch_shapes=[
            pltpu.VMEM((2 * half, BLOCK, D), F32),
            pltpu.VMEM((half, 8 * BLOCK, 2 * BLOCK), BF16),
            pltpu.SemaphoreType.DMA((half + 1,)),
        ],
        compiler_params=pltpu.CompilerParams(vmem_limit_bytes=32 * 1024 * 1024),
        name="grads",
        cost_estimate=pl.CostEstimate(
            flops=20 * half * 8 * BLOCK * BLOCK * D,
            bytes_accessed=14 * 1024 * 1024,
            transcendentals=0,
        ),
    )(glob, rand, qkg, v, hbm(p), hbm(dv))


def weight_kernel(count, nx, nz, ny, offset, me_ref, *refs):
    xs, parts, refs = refs[:count], refs[count : count + nx], refs[count + nx :]
    outs, (x_buf, cols, bufs, in_sems, x_sems, out_sems) = refs[:ny], refs[ny:]
    rows, size = cols.shape[0] // nz, bufs.shape[1]
    loads = []
    for n, part in enumerate(parts):
        head = pl.multiple_of(lax.rem(me_ref[0] + nx - n, nx) * D, D)
        for m in range(nz):
            first = pl.multiple_of((me_ref[1] ^ m) * rows, rows)
            loads.append(
                pltpu.make_async_copy(
                    part.at[pl.ds(first, rows)],
                    cols.at[pl.ds(m * rows, rows), pl.ds(head, D)],
                    in_sems.at[n * nz + m],
                )
            )
            loads[-1].start()
    x_loads = []
    for n in range(ny):
        tile_size = xs[0].shape[2] // ny
        at = pl.ds(pl.multiple_of(lax.rem(me_ref[2] + n, ny) * tile_size + offset, size), size)
        for m, x in enumerate(xs):
            load = pltpu.make_async_copy(
                x.at[0, :, at], x_buf.at[n, pl.ds(m * rows, rows)], x_sems.at[n * count + m]
            )
            load.start()
            x_loads.append(load)
    for load in loads:
        load.wait()
    stores = []
    for n, out in enumerate(outs):
        for load in x_loads[n * count : (n + 1) * count]:
            load.wait()
        bufs[n] = tn(x_buf[n], cols[...]).astype(BF16)
        stores.append(pltpu.make_async_copy(bufs.at[n], out, out_sems.at[n]))
        stores[n].start()
    for store in stores:
        store.wait()


def weight_call(me, xs, parts, nz, ny, half):
    nx, tokens = len(parts), parts[0].shape[0]
    features = xs[0].shape[2]
    size = features // ny // 2
    smem, hbm_spec = pl.BlockSpec(memory_space=pltpu.SMEM), pl.BlockSpec(memory_space=pl.ANY)
    return pl.pallas_call(
        functools.partial(weight_kernel, len(xs), nx, nz, ny, half * size),
        out_shape=[pltpu.HBM((size, nx * D), BF16)] * ny,
        in_specs=[smem] + [hbm_spec] * (len(xs) + nx),
        out_specs=[hbm_spec] * ny,
        scratch_shapes=[
            pltpu.VMEM((ny, tokens, size), BF16),
            pltpu.VMEM((tokens, nx * D), BF16),
            pltpu.VMEM((ny, size, nx * D), BF16),
            pltpu.SemaphoreType.DMA((nx * nz,)),
            pltpu.SemaphoreType.DMA((ny * len(xs),)),
            pltpu.SemaphoreType.DMA((ny,)),
        ],
        compiler_params=pltpu.CompilerParams(vmem_limit_bytes=24 * 1024 * 1024),
        name="weight",
        cost_estimate=pl.CostEstimate(
            flops=tokens * features * nx * D,
            bytes_accessed=4 * 1024 * 1024,
            transcendentals=0,
        ),
    )(me, *xs, *parts)


def sum_kernel(nz, nx, scale, in_ref, out_ref):
    for n in range(nz):
        total = in_ref[n].astype(F32)
        for r in range(1, in_ref.shape[0] // nz):
            total = total + in_ref[r * nz + n].astype(F32)
        total = total * scale
        for h in range(nx):
            c = (h * nz + n) * D
            out_ref[:, c : c + D] = total[:, h * D : (h + 1) * D]


def sum_call(array, nz, nx, scale):
    rows = array.shape[1]
    return pl.pallas_call(
        functools.partial(sum_kernel, nz, nx, scale),
        out_shape=jax.ShapeDtypeStruct((rows, nz * nx * D), F32),
        in_specs=[pl.BlockSpec(memory_space=pltpu.VMEM)],
        out_specs=pl.BlockSpec(memory_space=pltpu.VMEM),
        name="sum",
        cost_estimate=pl.CostEstimate(
            flops=array.size, bytes_accessed=2 * array.size, transcendentals=0
        ),
    )(array)


def swap(array, axes):
    return lax.all_to_all(array, axes, split_axis=0, concat_axis=0, tiled=True)


def shift(array, axis, n, size):
    return lax.ppermute(array, axis, [(i, (i + n) % size) for i in range(size)])


def per_device(queries, keys, values, out_grad, layer_input, global_blocks, random_blocks):
    local, features = layer_input.shape[1:]
    n_ctx, n_dp = lax.axis_size(CTX), lax.axis_size(DP)
    nx, ny, nz = lax.axis_size("x"), lax.axis_size("y"), lax.axis_size(("zl", "core"))
    nr = lax.axis_size(("zh", "x"))
    doc = local * n_ctx
    nb = doc // BLOCK
    scale = 1.0 / math.sqrt(D)
    me = [lax.axis_index("x"), lax.axis_index(("zl", "core")), lax.axis_index("y")]
    me = jnp.stack(me).astype(jnp.int32)

    qkg, v_in = pack((queries, keys, out_grad), (values,))
    qkg = swap(qkg, CTX)
    qkg, v_in, x_own = lax.optimization_barrier((qkg, v_in, layer_input))
    v_in = swap(v_in, CTX).reshape(n_ctx, 2, BLOCK, D)
    qkg = qkg.reshape(n_ctx, 6, BLOCK, D)
    x_zl = shift(x_own, "zl", 1, 2)
    x_core = shift(x_own, "core", 1, 2)
    probs, dv, *parts = probs_call(global_blocks, random_blocks, me, qkg, nx, scale)
    v_in, *parts = lax.optimization_barrier((v_in, *parts))
    parts = [part.reshape(doc // nx, D) for part in parts]
    parts = parts[:1] + [shift(parts[n], "x", n, nx) for n in range(1, nx)]
    qkv = grads_call(global_blocks, random_blocks, qkg, v_in, probs, dv, scale)
    qkv, x_zl, x_core, *parts = lax.optimization_barrier((qkv, x_zl, x_core, *parts))
    back = swap(qkv.reshape(n_ctx, 3 * local, D), CTX)
    x_both = vmem_pin(shift(x_zl, "core", 1, 2))
    xs = [hbm(x_own), hbm(x_core), hbm(x_zl), x_both]
    parts = [hbm(part) for part in parts]
    w_y = []
    for half in range(2):
        tiles = weight_call(me, xs, parts, nz, ny, half)
        tiles = [tiles[0]] + [shift(tiles[n], "y", n, ny) for n in range(1, ny)]
        w_y.append(sum(t.astype(F32) for t in tiles).astype(BF16))
    w_y = jnp.concatenate(w_y, axis=0)

    rows = features // (n_dp * n_ctx)
    w_y, back = lax.optimization_barrier((w_y, back))
    w_all = swap(w_y.reshape(nr * nz, rows, nx * D), ("zh", "x", "zl", "core"))
    w_out = sum_call(w_all, nz, nx, 1.0 / math.sqrt(doc * n_dp))
    dq, dk, dv_out = unpack(back, 3)
    return (dq, dk, dv_out, w_out)


def solution(mesh):
    fine = Mesh(mesh.devices.reshape(4, 2, 4, 2, 2), DP + CTX)
    tokens = P(DP, CTX, None)
    return jax.shard_map(
        per_device,
        mesh=fine,
        in_specs=(tokens,) * 5 + (P(DP, None), P(DP, None, None)),
        out_specs=(tokens, tokens, tokens, P(DP + CTX, None)),
        check_vma=False,
    )
```

```python
import functools
import math

import jax
import jax.numpy as jnp
from jax import lax
from jax.experimental import pallas as pl
from jax.experimental.pallas import tpu as pltpu
from jax.sharding import Mesh, PartitionSpec as P

D = 128
BLOCK = 128
F32 = jnp.float32
BF16 = jnp.bfloat16
LOG2E = 1.4426950408889634
DP = ("y", "zh")
CTX = ("x", "zl", "core")
NEG = float("-inf")


def vmem_pin(array):
    return pltpu.with_memory_space_constraint(array, pltpu.VMEM)


def hbm(array):
    return pltpu.with_memory_space_constraint(array, pltpu.HBM)


def pack_kernel(pieces, first_count, *refs):
    ins, (out, late_hbm, bufs, late, sems, late_sem) = refs[:-6], refs[-6:]
    count, rows = bufs.shape[:2]
    size = rows // pieces
    order = list(range(first_count, count)) + list(range(first_count))
    copies = {}
    for n in order:
        for m in range(pieces):
            at = pl.ds(m * size, size)
            copies[n, m] = pltpu.make_async_copy(ins[n].at[0, at], bufs.at[n, at], sems.at[n, m])
            copies[n, m].start()
    leave = pltpu.make_async_copy(late, late_hbm, late_sem)
    for n in order:
        to, i = (late, n - first_count) if n >= first_count else (out, n)
        for m in range(pieces):
            copies[n, m].wait()
            first = i * rows + m * size
            for h in range(out.shape[0]):
                to[h, first : first + size, :] = bufs[
                    n, m * size : (m + 1) * size, h * D : (h + 1) * D
                ]
        if n == count - 1:
            leave.start()
    leave.wait()


def pack(now, later):
    arrays = [*now, *later]
    rows, cols = arrays[0].shape[1:]
    heads, count, pieces = cols // D, len(arrays), 4
    late_shape = (heads, len(later) * rows, D)
    any_spec = pl.BlockSpec(memory_space=pl.ANY)
    return pl.pallas_call(
        functools.partial(pack_kernel, pieces, len(now)),
        out_shape=[
            jax.ShapeDtypeStruct((heads, len(now) * rows, D), BF16),
            pltpu.HBM(late_shape, BF16),
        ],
        in_specs=[any_spec] * count,
        out_specs=[pl.BlockSpec(memory_space=pltpu.VMEM), any_spec],
        scratch_shapes=[
            pltpu.VMEM((count, rows, cols), BF16),
            pltpu.VMEM(late_shape, BF16),
            pltpu.SemaphoreType.DMA((count, pieces)),
            pltpu.SemaphoreType.DMA,
        ],
        compiler_params=pltpu.CompilerParams(vmem_limit_bytes=24 * 1024 * 1024),
        name="pack",
        cost_estimate=pl.CostEstimate(
            flops=0, bytes_accessed=4 * rows * cols * count, transcendentals=0
        ),
    )(*[hbm(a) for a in arrays])


def unpack_kernel(count, src, *outs):
    rows = outs[0].shape[1]
    for n, out in enumerate(outs):
        for h in range(src.shape[0]):
            out[0, :, h * D : (h + 1) * D] = src[h, n * rows : (n + 1) * rows, :]


def unpack(array, count):
    heads, rows = array.shape[0], array.shape[1] // count
    return pl.pallas_call(
        functools.partial(unpack_kernel, count),
        out_shape=[jax.ShapeDtypeStruct((1, rows, heads * D), BF16)] * count,
        in_specs=[pl.BlockSpec(memory_space=pltpu.VMEM)],
        out_specs=[pl.BlockSpec(memory_space=pltpu.VMEM)] * count,
        compiler_params=pltpu.CompilerParams(vmem_limit_bytes=24 * 1024 * 1024),
        name="unpack",
        cost_estimate=pl.CostEstimate(
            flops=0, bytes_accessed=4 * rows * heads * D * count, transcendentals=0
        ),
    )(array)


def table_row(glob_ref, rand_ref, b, nb):
    left, right = b - 1, b + 1
    g0, g1 = glob_ref[0, 0], glob_ref[0, 1]
    idx = [
        jnp.maximum(left, 0),
        b,
        jnp.minimum(right, nb - 1),
        g0,
        g1,
        rand_ref[0, b, 0],
        rand_ref[0, b, 1],
        rand_ref[0, b, 2],
    ]

    def bias(c):
        return jnp.where(c, 0.0, NEG).astype(F32)

    biases = [
        bias(left >= 0),
        None,
        bias(right < nb),
        bias(jnp.abs(g0 - b) > 1),
        bias(jnp.abs(g1 - b) > 1),
        None,
        None,
        None,
    ]
    return idx, biases


def nt(a, b):
    return lax.dot_general(a, b, (((1,), (1,)), ((), ())), preferred_element_type=F32)


def tn(a, b):
    return lax.dot_general(a, b, (((0,), (0,)), ((), ())), preferred_element_type=F32)


def diag(a, b):
    zero = jnp.zeros_like(a)
    return jnp.concatenate(
        [jnp.concatenate([a, zero], axis=1), jnp.concatenate([zero, b], axis=1)], axis=0
    )


def pick(ref, idx, kind):
    return jnp.concatenate([ref[i // 2, 2 * kind + i % 2] for i in idx], axis=0)


def two(ref, u, kind):
    return diag(ref[u, 2 * kind], ref[u, 2 * kind + 1])


def tile(array, j, half):
    return array[j * D : (j + 1) * D, half * D : (half + 1) * D]


def add_tiles(acc, idx_pair, part):
    for j in range(8):
        for half, idx in enumerate(idx_pair):
            acc[idx[j]] += tile(part, j, half)


Q, K, G = 0, 1, 2
DQ, DK, DV = 0, 1, 2
LOADS = 4


def probs_kernel(nx, scale, glob_ref, rand_ref, me_ref, in_hbm, p_hbm, dv_ref, *rest):
    parts, (acc, buf, p_ref, sems, p_sems) = rest[:-5], rest[-5:]
    half_nb, nb = buf.shape[0], acc.shape[0]
    copies = []
    for kind in (K, Q, G):
        at = pl.ds(2 * kind, 2)
        for piece in range(LOADS):
            size = half_nb // LOADS
            rows = pl.ds(piece * size, size)
            copies.append(
                pltpu.make_async_copy(
                    in_hbm.at[rows, at], buf.at[rows, at], sems.at[kind * LOADS + piece]
                )
            )
            copies[-1].start()
    acc[...] = jnp.zeros_like(acc)
    for copy in copies:
        copy.wait()
    in_ref = buf

    def store(u):
        return pltpu.make_async_copy(p_ref.at[u], p_hbm.at[u], p_sems.at[u])

    def pair(u):
        rows = [table_row(glob_ref, rand_ref, 2 * u + half, nb) for half in range(2)]
        idx_pair = [row[0] for row in rows]
        keys = jnp.concatenate([pick(in_ref, idx, K) for idx in idx_pair], axis=1)
        s = nt(keys, two(in_ref, u, Q))
        ps = []
        for half, (_, biases) in enumerate(rows):
            tiles = [tile(s, j, half) for j in range(8)]
            tiles = [t if c is None else t + c for t, c in zip(tiles, biases)]
            top = jnp.max(functools.reduce(jnp.maximum, tiles), axis=0, keepdims=True)
            e = [jnp.exp2((t - top) * (scale * LOG2E)) for t in tiles]
            inv = 1.0 / jnp.sum(functools.reduce(jnp.add, e), axis=0, keepdims=True)
            ps.append(jnp.concatenate([(t * inv).astype(BF16) for t in e], axis=0))
        p = jnp.concatenate(ps, axis=1)
        p_ref[u] = p
        store(u).start()
        part = jnp.dot(p, two(in_ref, u, G), preferred_element_type=F32)
        add_tiles(acc, idx_pair, part)

    for u in range(half_nb):
        pair(u)
    dv_ref[...] = acc[...].astype(BF16).reshape(dv_ref.shape)
    size = parts[0].shape[0]
    for n, part in enumerate(parts):
        part[...] = dv_ref[pl.ds(lax.rem(me_ref[0] + n, nx) * size, size)]
    for u in range(half_nb):
        store(u).wait()


def probs_call(glob, rand, me, qkg, nx, scale):
    half = qkg.shape[0]
    smem, vmem = pl.BlockSpec(memory_space=pltpu.SMEM), pl.BlockSpec(memory_space=pltpu.VMEM)
    return pl.pallas_call(
        functools.partial(probs_kernel, nx, scale),
        out_shape=[
            pltpu.HBM((half, 8 * BLOCK, 2 * BLOCK), BF16),
            pltpu.HBM((half, 2, BLOCK, D), BF16),
        ]
        + [pltpu.HBM((half // nx, 2, BLOCK, D), BF16)] * nx,
        in_specs=[smem, smem, smem, pl.BlockSpec(memory_space=pl.ANY)],
        out_specs=[pl.BlockSpec(memory_space=pl.ANY)] + [vmem] * (1 + nx),
        scratch_shapes=[
            pltpu.VMEM((2 * half, BLOCK, D), F32),
            pltpu.VMEM((half, 6, BLOCK, D), BF16),
            pltpu.VMEM((half, 8 * BLOCK, 2 * BLOCK), BF16),
            pltpu.SemaphoreType.DMA((3 * LOADS,)),
            pltpu.SemaphoreType.DMA((half,)),
        ],
        compiler_params=pltpu.CompilerParams(vmem_limit_bytes=32 * 1024 * 1024),
        name="probs",
        cost_estimate=pl.CostEstimate(
            flops=16 * half * 8 * BLOCK * BLOCK * D,
            bytes_accessed=14 * 1024 * 1024,
            transcendentals=2 * half * 8 * BLOCK * BLOCK,
        ),
    )(glob, rand, me, hbm(qkg))


def grads_kernel(scale, glob_ref, rand_ref, in_ref, v_ref, p_hbm, dv_hbm, out_ref, *rest):
    acc, p_ref, sems = rest
    half_nb, nb = in_ref.shape[0], acc.shape[0]

    def load(u):
        return pltpu.make_async_copy(p_hbm.at[u], p_ref.at[u], sems.at[u])

    quarter = half_nb // 4
    for u in range(quarter):
        load(u).start()
    dv_load = pltpu.make_async_copy(dv_hbm, out_ref.at[:, pl.ds(2 * DV, 2)], sems.at[half_nb])
    acc[...] = jnp.zeros_like(acc)

    def pair(u):
        idx_pair = [table_row(glob_ref, rand_ref, 2 * u + half, nb)[0] for half in range(2)]
        vals = jnp.concatenate([pick(v_ref, idx, 0) for idx in idx_pair], axis=1)
        dp = nt(vals, two(in_ref, u, G))
        both = []
        for half, idx in enumerate(idx_pair):
            ps = [tile(p_ref[u], j, half).astype(F32) for j in range(8)]
            ts = [ps[j] * tile(dp, j, half) for j in range(8)]
            delta = jnp.sum(functools.reduce(jnp.add, ts), axis=0, keepdims=True)
            ds = jnp.concatenate([(t - x * delta).astype(BF16) for t, x in zip(ts, ps)], axis=0)
            both.append(ds)
            out_ref[u, 2 * DQ + half] = (tn(ds, pick(in_ref, idx, K)) * scale).astype(BF16)
        ds = jnp.concatenate(both, axis=1)
        part = jnp.dot(ds, two(in_ref, u, Q), preferred_element_type=F32)
        add_tiles(acc, idx_pair, part)

    def batch(first, size, after):
        for u in range(size):
            load(first + u).wait()
        for u in range(after):
            load(first + size + u).start()
        for u in range(size):
            pair(first + u)

    batch(0, quarter, 3 * quarter)
    dv_load.start()
    batch(quarter, 3 * quarter, 0)

    out_ref[:, 2 * DK : 2 * DK + 2] = (acc[...] * scale).astype(BF16).reshape(dv_hbm.shape)
    dv_load.wait()


def grads_call(glob, rand, qkg, v, p, dv, scale):
    half = qkg.shape[0]
    smem, vmem = pl.BlockSpec(memory_space=pltpu.SMEM), pl.BlockSpec(memory_space=pltpu.VMEM)
    return pl.pallas_call(
        functools.partial(grads_kernel, scale),
        out_shape=pltpu.HBM((half, 6, BLOCK, D), BF16),
        in_specs=[smem, smem, vmem, vmem] + [pl.BlockSpec(memory_space=pl.ANY)] * 2,
        out_specs=vmem,
        scratch_shapes=[
            pltpu.VMEM((2 * half, BLOCK, D), F32),
            pltpu.VMEM((half, 8 * BLOCK, 2 * BLOCK), BF16),
            pltpu.SemaphoreType.DMA((half + 1,)),
        ],
        compiler_params=pltpu.CompilerParams(vmem_limit_bytes=32 * 1024 * 1024),
        name="grads",
        cost_estimate=pl.CostEstimate(
            flops=20 * half * 8 * BLOCK * BLOCK * D,
            bytes_accessed=14 * 1024 * 1024,
            transcendentals=0,
        ),
    )(glob, rand, qkg, v, hbm(p), hbm(dv))


def weight_kernel(count, nx, nz, ny, offset, me_ref, *refs):
    xs, parts, refs = refs[:count], refs[count : count + nx], refs[count + nx :]
    outs, (x_buf, cols, bufs, in_sems, x_sems, out_sems) = refs[:ny], refs[ny:]
    rows, size = cols.shape[0] // nz, bufs.shape[1]
    loads = []
    for n, part in enumerate(parts):
        head = pl.multiple_of(lax.rem(me_ref[0] + nx - n, nx) * D, D)
        for m in range(nz):
            first = pl.multiple_of((me_ref[1] ^ m) * rows, rows)
            loads.append(
                pltpu.make_async_copy(
                    part.at[pl.ds(first, rows)],
                    cols.at[pl.ds(m * rows, rows), pl.ds(head, D)],
                    in_sems.at[n * nz + m],
                )
            )
            loads[-1].start()
    x_loads = []
    for n in range(ny):
        tile_size = xs[0].shape[2] // ny
        at = pl.ds(pl.multiple_of(lax.rem(me_ref[2] + n, ny) * tile_size + offset, size), size)
        for m, x in enumerate(xs):
            load = pltpu.make_async_copy(
                x.at[0, :, at], x_buf.at[n, pl.ds(m * rows, rows)], x_sems.at[n * count + m]
            )
            load.start()
            x_loads.append(load)
    for load in loads:
        load.wait()
    stores = []
    for n, out in enumerate(outs):
        for load in x_loads[n * count : (n + 1) * count]:
            load.wait()
        bufs[n] = tn(x_buf[n], cols[...]).astype(BF16)
        stores.append(pltpu.make_async_copy(bufs.at[n], out, out_sems.at[n]))
        stores[n].start()
    for store in stores:
        store.wait()


def weight_call(me, xs, parts, nz, ny, half):
    nx, tokens = len(parts), parts[0].shape[0]
    features = xs[0].shape[2]
    size = features // ny // 2
    smem, hbm_spec = pl.BlockSpec(memory_space=pltpu.SMEM), pl.BlockSpec(memory_space=pl.ANY)
    return pl.pallas_call(
        functools.partial(weight_kernel, len(xs), nx, nz, ny, half * size),
        out_shape=[pltpu.HBM((size, nx * D), BF16)] * ny,
        in_specs=[smem] + [hbm_spec] * (len(xs) + nx),
        out_specs=[hbm_spec] * ny,
        scratch_shapes=[
            pltpu.VMEM((ny, tokens, size), BF16),
            pltpu.VMEM((tokens, nx * D), BF16),
            pltpu.VMEM((ny, size, nx * D), BF16),
            pltpu.SemaphoreType.DMA((nx * nz,)),
            pltpu.SemaphoreType.DMA((ny * len(xs),)),
            pltpu.SemaphoreType.DMA((ny,)),
        ],
        compiler_params=pltpu.CompilerParams(vmem_limit_bytes=24 * 1024 * 1024),
        name="weight",
        cost_estimate=pl.CostEstimate(
            flops=tokens * features * nx * D,
            bytes_accessed=4 * 1024 * 1024,
            transcendentals=0,
        ),
    )(me, *xs, *parts)


def sum_kernel(nz, nx, scale, in_ref, out_ref):
    for n in range(nz):
        total = in_ref[n].astype(F32)
        for r in range(1, in_ref.shape[0] // nz):
            total = total + in_ref[r * nz + n].astype(F32)
        total = total * scale
        for h in range(nx):
            c = (h * nz + n) * D
            out_ref[:, c : c + D] = total[:, h * D : (h + 1) * D]


def sum_call(array, nz, nx, scale):
    rows = array.shape[1]
    return pl.pallas_call(
        functools.partial(sum_kernel, nz, nx, scale),
        out_shape=jax.ShapeDtypeStruct((rows, nz * nx * D), F32),
        in_specs=[pl.BlockSpec(memory_space=pltpu.VMEM)],
        out_specs=pl.BlockSpec(memory_space=pltpu.VMEM),
        name="sum",
        cost_estimate=pl.CostEstimate(
            flops=array.size, bytes_accessed=2 * array.size, transcendentals=0
        ),
    )(array)


def swap(array, axes):
    return lax.all_to_all(array, axes, split_axis=0, concat_axis=0, tiled=True)


def shift(array, axis, n, size):
    return lax.ppermute(array, axis, [(i, (i + n) % size) for i in range(size)])


def per_device(queries, keys, values, out_grad, layer_input, global_blocks, random_blocks):
    local, features = layer_input.shape[1:]
    n_ctx, n_dp = lax.axis_size(CTX), lax.axis_size(DP)
    nx, ny, nz = lax.axis_size("x"), lax.axis_size("y"), lax.axis_size(("zl", "core"))
    nr = lax.axis_size(("zh", "x"))
    doc = local * n_ctx
    nb = doc // BLOCK
    scale = 1.0 / math.sqrt(D)
    me = [lax.axis_index("x"), lax.axis_index(("zl", "core")), lax.axis_index("y")]
    me = jnp.stack(me).astype(jnp.int32)

    qkg, v_in = pack((queries, keys, out_grad), (values,))
    qkg = swap(qkg, CTX)
    qkg, v_in, x_own = lax.optimization_barrier((qkg, v_in, layer_input))
    v_in = swap(v_in, CTX).reshape(n_ctx, 2, BLOCK, D)
    qkg = qkg.reshape(n_ctx, 6, BLOCK, D)
    x_zl = shift(x_own, "zl", 1, 2)
    x_core = shift(x_own, "core", 1, 2)
    probs, dv, *parts = probs_call(global_blocks, random_blocks, me, qkg, nx, scale)
    v_in, *parts = lax.optimization_barrier((v_in, *parts))
    parts = [part.reshape(doc // nx, D) for part in parts]
    parts = parts[:1] + [shift(parts[n], "x", n, nx) for n in range(1, nx)]
    qkv = grads_call(global_blocks, random_blocks, qkg, v_in, probs, dv, scale)
    qkv, x_zl, x_core, *parts = lax.optimization_barrier((qkv, x_zl, x_core, *parts))
    back = swap(qkv.reshape(n_ctx, 3 * local, D), CTX)
    x_both = vmem_pin(shift(x_zl, "core", 1, 2))
    xs = [hbm(x_own), hbm(x_core), hbm(x_zl), x_both]
    parts = [vmem_pin(part) if n == 1 else hbm(part) for n, part in enumerate(parts)]
    w_y = []
    for half in range(2):
        tiles = weight_call(me, xs, parts, nz, ny, half)
        tiles = [tiles[0]] + [shift(tiles[n], "y", n, ny) for n in range(1, ny)]
        w_y.append(sum(t.astype(F32) for t in tiles).astype(BF16))
    w_y = jnp.concatenate(w_y, axis=0)

    rows = features // (n_dp * n_ctx)
    w_y, back = lax.optimization_barrier((w_y, back))
    w_all = swap(w_y.reshape(nr * nz, rows, nx * D), ("zh", "x", "zl", "core"))
    w_out = sum_call(w_all, nz, nx, 1.0 / math.sqrt(doc * n_dp))
    dq, dk, dv_out = unpack(back, 3)
    return (dq, dk, dv_out, w_out)


def solution(mesh):
    fine = Mesh(mesh.devices.reshape(4, 2, 4, 2, 2), DP + CTX)
    tokens = P(DP, CTX, None)
    return jax.shard_map(
        per_device,
        mesh=fine,
        in_specs=(tokens,) * 5 + (P(DP, None), P(DP, None, None)),
        out_specs=(tokens, tokens, tokens, P(DP + CTX, None)),
        check_vma=False,
    )
```
